256 devices in a mesh: sec: 2 (over z_hi), seq: 16 (over y, z_lo), tp: 8 (over x, core).
Axes of the slice: x: 4, y: 4, z: 8 (z_hi: 2, z_lo: 4; z = z_hi * 4 + z_lo), core: 2. Of those that a mesh axis runs over, the one named last changes fastest.
Arguments:
- hidden_context: bfloat16 [8192, 8192], P(('sec', 'seq'), 'tp')
- hidden_rows: bfloat16 [512, 8192], P(('sec', 'seq'), 'tp')
- norm_gain: float32 [8192], replicated, may hold values from 0.25 to 2
- key_value_weight: bfloat16 [8192, 2, 1024], P(None, None, 'tp'), may hold values from -0.0625 to 0.0625
- value_bias: float32 [1024], P('tp'), may hold values from -4 to 4
- query_context: bfloat16 [8192, 8192], P(('sec', 'seq'), 'tp')
- query_rows: bfloat16 [512, 8192], P(('sec', 'seq'), 'tp')
- context_length: int32 [512], P(('sec', 'seq')), may hold values from 1 to 8192, as said below
- row_node: int32 [512], replicated, may hold values from 0 to 255, never falling along the last dimension, each value on 1 to 4 neighbouring positions
Outputs:
- prefill_attended: bfloat16 [8192, 8192], P(('sec', 'seq'), 'tp')
- decode_attended: bfloat16 [512, 8192], P(('sec', 'seq'), 'tp')
The draws below stay inside these ranges and needn't reach their ends.
Inputs may be any that keep to these rules, and one draw needn't show every extreme that they name: `context_length`: some row sees the whole context of 8192 tokens. `row_node`: never falls; each node holds 1 to 4 consecutive rows, and some node exactly 4.
All inputs are finite; a program needn't handle non-finite values.
Results may differ from the reference program's by a relative error of at most 0.012.
The reference program's roundings to bfloat16 on the way count: a program that leaves them out, or rounds other values in their place, can miss the bound.
Values may be sent and summed in bfloat16 or wider, within the bound.
No kernel may reach another device: no remote copies, remote signals or barrier semaphores. Data moves between devices by JAX's collectives and lax.ppermute only.
A program may use at most 64 MiB of HBM per device.

```python
import math
import jax
import jax.numpy as jnp
import numpy as np
from jax import lax

D = 8192
H = 64
KVH = 8
HD = 128
TOK_DEV = 256
ROW_DEV = 16
STEPS = 4
CONTEXT = 8192
ROWS = 512
NODES = 256


def feature_scales(key):
    return jnp.exp(jax.random.uniform(key, (D,), minval=math.log(0.5), maxval=math.log(5.0)))


def scaled_states(base, key, count, columns):
    row_scales = jnp.exp(jax.random.uniform(key, (count, 1), minval=math.log(0.5), maxval=math.log(5.0)))
    return (base * row_scales * columns).astype(jnp.bfloat16)


def draw_hidden_context(key, part):
    columns = feature_scales(key)
    key = jax.random.fold_in(key, 11)
    first, second = jax.random.split(key)
    base = jax.random.normal(first, (CONTEXT, D))
    return scaled_states(base, second, CONTEXT, columns)


def draw_hidden_rows(key, part):
    columns = feature_scales(key)
    key = jax.random.fold_in(key, 12)
    first, second = jax.random.split(key)
    base = jax.random.normal(first, (ROWS, D))
    return scaled_states(base, second, ROWS, columns)


def draw_query_context(key, part):
    key = jax.random.fold_in(key, 13)
    first = jax.random.fold_in(key, 0)
    base = jax.random.normal(first, (CONTEXT, H, HD))
    return base.reshape(CONTEXT, H * HD).astype(jnp.bfloat16)


def draw_query_rows(key, part):
    key = jax.random.fold_in(key, 14)
    first = jax.random.fold_in(key, 0)
    base = jax.random.normal(first, (ROWS, H, HD))
    return base.reshape(ROWS, H * HD).astype(jnp.bfloat16)


def draw_context_length(key, part):
    key = jax.random.fold_in(key, 15)
    first, second, third = jax.random.split(key, 3)
    raw = jax.random.randint(first, (ROWS,), 0, CONTEXT)
    power = jax.random.randint(second, (ROWS,), 0, 12)
    lengths = 1 + raw // jnp.left_shift(jnp.ones((ROWS,), jnp.int32), power)
    chosen = jax.random.randint(third, (), 0, ROWS)
    lengths = jnp.where(jnp.arange(ROWS) == chosen, CONTEXT, lengths)
    return lengths.astype(jnp.int32)


def level_of(own_key, dims, cuts, least, high):
    def one(position, parts):
        heights = jax.random.uniform(jax.random.fold_in(jax.random.fold_in(own_key, 6), position), (parts,), jnp.float32, least / len(cuts), high / len(cuts))
        return jnp.repeat(jnp.exp(heights), dims[position] // parts).reshape((-1,) + (1,) * (len(dims) - position - 1))

    loudness = one(*cuts[0])
    for cut in cuts[1:]:
        loudness = loudness * one(*cut)
    return loudness


def split_up(amount, total, bound, skew):
    portions = [(1 << 20) // math.isqrt(rank ** skew) + 1 for rank in range(2, amount + 1)]
    spare, holding = total - bound - (amount - 1), [1] * (amount - 1)
    while spare > 0:
        free = [i for i in range(amount - 1) if holding[i] < bound]
        pool, left = sum([portions[i] for i in free]), spare
        for i in free:
            addition = min(bound - holding[i], max(1, left * portions[i] // pool), spare)
            holding[i] = holding[i] + addition
            spare = spare - addition
    return np.array([bound] + holding)


def ragged(key, number_of, total, most, lean):
    if number_of == 2:
        one = jax.random.randint(key, (), max(1, total - most), min(most, total - 1) + 1)
        return jnp.stack([one, total - one])
    tallies = jnp.asarray(split_up(number_of, total, most, lean), jnp.int32)
    couples = (number_of - 1) // 2
    giver, sink = tallies[1:1 + 2 * couples:2], tallies[2:2 + 2 * couples:2]
    room = jnp.minimum(giver - 1, most - sink)
    passed = jax.random.randint(jax.random.fold_in(key, 1), (couples,), 0, 1 << 20) % (room + 1)
    tallies = tallies.at[1:1 + 2 * couples:2].set(giver - passed).at[2:2 + 2 * couples:2].set(sink + passed)
    return tallies[jax.random.permutation(jax.random.fold_in(key, 2), number_of)]


def scatter_about(key, extent, deviation, bound, cuts=(), kind=jnp.bfloat16):
    entries = jax.random.normal(key, extent, jnp.float32) * deviation
    if len(cuts) > 0:
        entries = level_of(key, extent, cuts, -0.22, 0.18) * entries
    return jnp.clip(entries, min=-bound, max=bound).astype(kind)


def setup_inputs(seed: int = 0) -> dict:
    splits = jax.random.split(jax.random.key(seed), 10)
    return {
        "hidden_context": draw_hidden_context(jax.random.fold_in(splits[9], 71), 0),
        "hidden_rows": draw_hidden_rows(jax.random.fold_in(splits[9], 71), 0),
        "norm_gain": jnp.clip(jax.random.uniform(splits[2], (D,), jnp.float32, 0.25, 2.0), 0.25, 2.0),
        "key_value_weight": scatter_about(splits[3], (D, 2, KVH * HD), D ** -0.5, 0.0625, ((2, 8),)),
        "value_bias": scatter_about(splits[4], (KVH * HD,), 1.0, 4.0, ((0, 8),), jnp.float32),
        "query_context": draw_query_context(jax.random.fold_in(splits[9], 71), 0),
        "query_rows": draw_query_rows(jax.random.fold_in(splits[9], 71), 0),
        "context_length": draw_context_length(jax.random.fold_in(splits[9], 71), 0),
        "row_node": jnp.searchsorted(jnp.cumsum(ragged(splits[8], NODES, ROWS, STEPS, 0)), jnp.arange(ROWS), side="right").astype(jnp.int32),
    }


def normed_pair(hidden, norm_gain, key_value_weight, value_bias):
    wide = hidden.astype(jnp.float32)
    inverse = lax.rsqrt(lax.optimization_barrier(jnp.sum(wide * wide, axis=1, keepdims=True)) / D + 1e-06)
    scaled = (wide * norm_gain).astype(jnp.bfloat16)
    keys = jnp.dot(scaled, key_value_weight[:, 0, :], preferred_element_type=jnp.float32) * inverse
    values = jnp.dot(scaled, key_value_weight[:, 1, :], preferred_element_type=jnp.float32) * inverse + value_bias
    return (keys.astype(jnp.bfloat16), values.astype(jnp.bfloat16))

def attend(queries, keys, values, allowed):
    scores = jnp.einsum('rkgd,nkd->kgrn', queries.astype(jnp.float32), keys.astype(jnp.float32)) / math.sqrt(HD)
    scores = jnp.where(allowed, scores, -1e+30)
    highest = lax.optimization_barrier(jnp.max(scores, axis=-1, keepdims=True))
    weights = jnp.where(allowed, jnp.exp(scores - highest), 0.0)
    total = lax.optimization_barrier(jnp.sum(weights, axis=-1))
    rounded = lax.optimization_barrier(weights.astype(jnp.bfloat16))
    mixed = jnp.einsum('kgrn,nkd->kgrd', rounded.astype(jnp.float32), values.astype(jnp.float32))
    result = mixed / total[..., None]
    result = jnp.transpose(result, (2, 0, 1, 3))
    return result.reshape(result.shape[0], H * HD).astype(jnp.bfloat16)

def reference(hidden_context, hidden_rows, norm_gain, key_value_weight, value_bias, query_context, query_rows, context_length, row_node):
    group = H // KVH
    key_context, value_context = normed_pair(hidden_context, norm_gain, key_value_weight, value_bias)
    key_rows, value_rows = normed_pair(hidden_rows, norm_gain, key_value_weight, value_bias)
    keys_three = key_context.reshape(CONTEXT, KVH, HD)
    values_three = value_context.reshape(CONTEXT, KVH, HD)
    key_positions = jnp.arange(CONTEXT, dtype=jnp.int32)

    def prefill_block(number):
        begin = (number * TOK_DEV).astype(jnp.int32)
        queries = lax.dynamic_slice_in_dim(query_context, begin, TOK_DEV, 0).reshape(TOK_DEV, KVH, group, HD)
        positions = begin + jnp.arange(TOK_DEV, dtype=jnp.int32)
        allowed = key_positions[None, :] <= positions[:, None]
        return attend(queries, keys_three, values_three, allowed)
    prefill_attended = lax.map(prefill_block, jnp.arange(CONTEXT // TOK_DEV, dtype=jnp.int32)).reshape(CONTEXT, H * HD)
    all_keys = jnp.concatenate([key_context, key_rows], axis=0).reshape(CONTEXT + ROWS, KVH, HD)
    all_values = jnp.concatenate([value_context, value_rows], axis=0).reshape(CONTEXT + ROWS, KVH, HD)
    row_index = jnp.arange(ROWS, dtype=jnp.int32)

    def decode_block(number):
        begin = (number * ROW_DEV).astype(jnp.int32)
        queries = lax.dynamic_slice_in_dim(query_rows, begin, ROW_DEV, 0).reshape(ROW_DEV, KVH, group, HD)
        positions = begin + jnp.arange(ROW_DEV, dtype=jnp.int32)
        lengths = lax.dynamic_slice_in_dim(context_length, begin, ROW_DEV, 0)
        nodes = lax.dynamic_slice_in_dim(row_node, begin, ROW_DEV, 0)
        context_ok = key_positions[None, :] < lengths[:, None]
        appended_ok = (row_index[None, :] <= positions[:, None]) & (row_node[None, :] == nodes[:, None])
        allowed = jnp.concatenate([context_ok, appended_ok], axis=1)
        return attend(queries, all_keys, all_values, allowed)
    decode_attended = lax.map(decode_block, jnp.arange(ROWS // ROW_DEV, dtype=jnp.int32)).reshape(ROWS, H * HD)
    return (prefill_attended, decode_attended)
```

```python
import functools
import math

import jax
import jax.numpy as jnp
from jax import lax
from jax.experimental import pallas as pl
from jax.experimental.pallas import tpu as pltpu
from jax.sharding import PartitionSpec as P

D = 8192
H = 64
KVH = 8
HD = 128
STEPS = 4
GROUP = H // KVH

PLACE = ("sec", "seq")
RING_Z, RING_Y, RUN = 8, 4, 4
TOK = 256
ROW = 16
BOTH = TOK + ROW
TOP = 128
LOWEST = -1e30
SCALE = math.log2(math.e) / math.sqrt(HD)
VMEM = 48 * 1024 * 1024


def place_of(y, z):
    return (z // RUN) * (RING_Y * RUN) + y * RUN + z % RUN


def move(block, dz, dy):
    route = [
        (place_of(y, z), place_of((y + dy) % RING_Y, (z + dz) % RING_Z))
        for y in range(RING_Y)
        for z in range(RING_Z)
    ]
    return lax.ppermute(block, PLACE, route)


def move_x(block, step):
    return lax.ppermute(block, "tp", [(i, (i + 2 * step) % 8) for i in range(8)])


def swap_core(block):
    return lax.ppermute(block, "tp", [(i, i ^ 1) for i in range(8)])


def project_kernel(count, first, last, owners, *refs):
    refs = list(refs)
    pieces = [refs.pop(0) for _ in range(count)]
    weights = [refs.pop(0) for _ in range(count)]
    gain = refs.pop(0)
    if not first:
        product_in, squares_in = refs.pop(0), refs.pop(0)
    if last:
        bias = refs.pop(0)
    product = jnp.zeros((BOTH, 2 * HD), jnp.float32) if first else product_in[...]
    squares = jnp.zeros((BOTH, HD), jnp.float32) if first else squares_in[...]
    for number in range(count):
        own_gain = gain[pl.ds(owners[number], 1), :]
        for begin in range(0, 1024, 256):
            wide = pieces[number][:, begin : begin + 256].astype(jnp.float32)
            squared = wide * wide
            squares = squares + (squared[:, :HD] + squared[:, HD:])
            scaled = (wide * own_gain[:, begin : begin + 256]).astype(jnp.bfloat16)
            product = product + jnp.dot(
                scaled,
                weights[number][begin : begin + 256, :],
                preferred_element_type=jnp.float32,
            )
    if not last:
        refs[0][...] = product
        refs[1][...] = squares
        return
    inverse = lax.rsqrt(jnp.sum(squares, axis=1, keepdims=True) / D + 1e-06)
    keys = (product[:, :HD] * inverse).astype(jnp.bfloat16)
    values = (product[:, HD:] * inverse + bias[...]).astype(jnp.bfloat16)
    refs[0][:, :HD] = keys[:TOK]
    refs[0][:, HD:] = values[:TOK]
    refs[1][:, :HD] = keys[TOK:]
    refs[1][:, HD:] = values[TOK:]


def project(pieces, owners, weights, gain, state, bias):
    count = len(pieces)
    first, last = state is None, bias is not None

    def whole(array):
        return pl.BlockSpec(array.shape, lambda i, own: (0,) * array.ndim)

    operands = list(pieces) + [weights] * count + [gain]
    specs = [whole(piece) for piece in pieces]
    for number in range(count):
        specs.append(
            pl.BlockSpec((1024, 2 * HD), functools.partial(lambda j, i, own: (own[j], 0), number))
        )
    specs.append(whole(gain))
    if not first:
        operands += list(state)
        specs += [whole(array) for array in state]
    if last:
        operands.append(bias)
        specs.append(whole(bias))
        shapes = [
            jax.ShapeDtypeStruct((TOK, 2 * HD), jnp.bfloat16),
            jax.ShapeDtypeStruct((ROW, 2 * HD), jnp.bfloat16),
        ]
    else:
        shapes = [
            jax.ShapeDtypeStruct((BOTH, 2 * HD), jnp.float32),
            jax.ShapeDtypeStruct((BOTH, HD), jnp.float32),
        ]
    return pl.pallas_call(
        functools.partial(project_kernel, count, first, last),
        grid_spec=pltpu.PrefetchScalarGridSpec(
            num_scalar_prefetch=1,
            grid=(1,),
            in_specs=specs,
            out_specs=[whole(shape) for shape in shapes],
        ),
        out_shape=shapes,
        compiler_params=pltpu.CompilerParams(vmem_limit_bytes=VMEM),
        cost_estimate=pl.CostEstimate(
            flops=count * BOTH * 1024 * 512, bytes_accessed=count * 1100000, transcendentals=0
        ),
    )(owners, *operands)


def attend(queries, keys, values, allowed, top_ref, mixed_ref):
    parts = []
    highest = None
    for number in range(len(keys)):
        scores = lax.dot_general(
            queries, keys[number], (((1,), (1,)), ((), ())), preferred_element_type=jnp.float32
        )
        scores = scores * SCALE
        if allowed is not None:
            scores = jnp.where(allowed[number], scores, LOWEST)
        parts.append(scores)
        for begin in range(0, scores.shape[1], HD):
            piece = scores[:, begin : begin + HD]
            highest = piece if highest is None else jnp.maximum(highest, piece)
    before = top_ref[...]
    top = jnp.maximum(before, jnp.max(highest, axis=1, keepdims=True))
    factor = jnp.exp2(before - top)
    mixed = mixed_ref[...] * jnp.concatenate([factor, factor], axis=1)
    for number in range(len(keys)):
        width = parts[number].shape[1]
        lifted = jnp.concatenate([top] * (width // HD), axis=1)
        weight = jnp.exp2(parts[number] - lifted)
        if allowed is not None:
            weight = jnp.where(allowed[number], weight, 0.0)
        mixed = mixed + jnp.dot(
            weight.astype(jnp.bfloat16), values[number], preferred_element_type=jnp.float32
        )
    top_ref[...] = top
    mixed_ref[...] = mixed


def stage_kernel(lines, sizes, first, last, info, *refs):
    refs = list(refs)
    blocks = [refs.pop(0) for _ in sizes]
    query, query_rows, lengths = refs.pop(0), refs.pop(0), refs.pop(0)
    if first:
        extra, extra_ok = refs.pop(0), refs.pop(0)
    else:
        top_in, mixed_in, top_rows_in, mixed_rows_in = (refs.pop(0) for _ in range(4))
    if last:
        out, out_rows = refs.pop(0), refs.pop(0)
        keys, values, top_ref, mixed_ref, top_rows, mixed_rows = refs
    else:
        top_ref, mixed_ref, top_rows, mixed_rows, keys, values = refs
    step = pl.program_id(0)
    place, longest = info[0], info[1]

    @pl.when(step == 0)
    def _():
        number = 0
        for block, size in zip(blocks, sizes):
            for begin in range(0, size, TOK):
                spot = pl.multiple_of(info[8 + number] * TOK, TOK)
                keys[pl.ds(spot, TOK), :] = block[begin : begin + TOK, :HD]
                values[pl.ds(spot, TOK), :HD] = block[begin : begin + TOK, HD:]
                number += 1
        values[:, HD:] = jnp.ones((values.shape[0], HD), jnp.bfloat16)

    def parts_of(group):
        spans = [slice((4 * group + i) * TOK, (4 * group + i + 1) * TOK) for i in range(4)]
        return [keys[span, :] for span in spans], [values[span, :] for span in spans]

    @pl.when(step < GROUP)
    def _():
        if first:
            top_ref[...] = jnp.full(top_ref.shape, LOWEST, jnp.float32)
            mixed_ref[...] = jnp.zeros(mixed_ref.shape, jnp.float32)
        else:
            top_ref[...] = top_in[...]
            mixed_ref[...] = mixed_in[...]
        for group in range(2 * lines):
            number = info[2 + group]

            @pl.when(number < place // RUN)
            def _(group=group):
                some_keys, some_values = parts_of(group)
                attend(query[...], some_keys, some_values, None, top_ref, mixed_ref)

            if first:

                @pl.when(number == place // RUN)
                def _(group=group):
                    some_keys, some_values = parts_of(group)
                    tokens = lax.broadcasted_iota(jnp.int32, (TOK, TOK), 0) + (place % RUN) * TOK
                    offsets = lax.broadcasted_iota(jnp.int32, (TOK, TOK), 1)
                    allowed = [offsets + i * TOK <= tokens for i in range(4)]
                    attend(query[...], some_keys, some_values, allowed, top_ref, mixed_ref)

        if last:
            mixed = mixed_ref[...]
            out[...] = (mixed[:, :HD] / mixed[:, HD:]).astype(out.dtype)

    @pl.when(step == GROUP)
    def _():
        if first:
            top_rows[...] = jnp.full(top_rows.shape, LOWEST, jnp.float32)
            mixed_rows[...] = jnp.zeros(mixed_rows.shape, jnp.float32)
            extra_values = jnp.concatenate(
                [extra[:, HD:], jnp.ones((extra.shape[0], HD), jnp.bfloat16)], axis=1
            )
            attend(
                query_rows[...],
                [extra[:, :HD]],
                [extra_values],
                [extra_ok[...] > 0],
                top_rows,
                mixed_rows,
            )
        else:
            top_rows[...] = top_rows_in[...]
            mixed_rows[...] = mixed_rows_in[...]
        for group in range(2 * lines):
            number = info[2 + group]

            @pl.when(number * (RUN * TOK) < longest)
            def _(group=group, number=number):
                some_keys, some_values = parts_of(group)
                reach = lengths[...] - number * (RUN * TOK)
                reach = jnp.concatenate([reach, reach], axis=1)
                offsets = lax.broadcasted_iota(jnp.int32, reach.shape, 1)
                allowed = [offsets + i * TOK < reach for i in range(4)]
                attend(query_rows[...], some_keys, some_values, allowed, top_rows, mixed_rows)

        if last:
            mixed = mixed_rows[...]
            out_rows[...] = (mixed[:, :HD] / mixed[:, HD:]).astype(out_rows.dtype)


def stage(lines, info, blocks, query, query_rows, lengths, extra, state, last):
    first = state is None
    sizes = [block.shape[0] for block in blocks]

    def whole(array):
        return pl.BlockSpec(array.shape, lambda i, info: (0,) * len(array.shape))

    def down(width):
        return pl.BlockSpec((TOK, width), lambda i, info: (jnp.minimum(i, GROUP - 1), 0))

    across = pl.BlockSpec((TOK, HD), lambda i, info: (0, jnp.minimum(i, GROUP - 1)))
    operands = list(blocks) + [query, query_rows, lengths]
    specs = [whole(block) for block in blocks] + [across, whole(query_rows), whole(lengths)]
    state_shapes = [
        jax.ShapeDtypeStruct((GROUP * TOK, HD), jnp.float32),
        jax.ShapeDtypeStruct((GROUP * TOK, 2 * HD), jnp.float32),
        jax.ShapeDtypeStruct((GROUP * ROW, HD), jnp.float32),
        jax.ShapeDtypeStruct((GROUP * ROW, 2 * HD), jnp.float32),
    ]
    state_specs = [down(HD), down(2 * HD), whole(state_shapes[2]), whole(state_shapes[3])]
    if first:
        operands += list(extra)
        specs += [whole(array) for array in extra]
    else:
        operands += list(state)
        specs += state_specs
    scratch = [
        pltpu.VMEM((lines * RING_Z * TOK, HD), jnp.bfloat16),
        pltpu.VMEM((lines * RING_Z * TOK, 2 * HD), jnp.bfloat16),
    ]
    if last:
        shapes = [
            jax.ShapeDtypeStruct((TOK, GROUP * HD), jnp.bfloat16),
            jax.ShapeDtypeStruct((GROUP * ROW, HD), jnp.bfloat16),
        ]
        out_specs = [across, whole(shapes[1])]
        scratch += [
            pltpu.VMEM((TOK, HD), jnp.float32),
            pltpu.VMEM((TOK, 2 * HD), jnp.float32),
            pltpu.VMEM((GROUP * ROW, HD), jnp.float32),
            pltpu.VMEM((GROUP * ROW, 2 * HD), jnp.float32),
        ]
    else:
        shapes, out_specs = state_shapes, state_specs
    work = lines * RING_Z * TOK * TOK * GROUP
    return pl.pallas_call(
        functools.partial(stage_kernel, lines, sizes, first, last),
        grid_spec=pltpu.PrefetchScalarGridSpec(
            num_scalar_prefetch=1,
            grid=(GROUP + 1,),
            in_specs=specs,
            out_specs=out_specs,
            scratch_shapes=scratch,
        ),
        out_shape=shapes,
        compiler_params=pltpu.CompilerParams(vmem_limit_bytes=VMEM),
        cost_estimate=pl.CostEstimate(
            flops=work * 4 * HD * 2, bytes_accessed=4000000, transcendentals=work
        ),
    )(info, *operands)


def per_device(
    hidden_context,
    hidden_rows,
    norm_gain,
    key_value_weight,
    value_bias,
    query_context,
    query_rows,
    context_length,
    row_node,
):
    weights = key_value_weight.reshape(D, 2 * HD)
    gain = norm_gain.reshape(8, 1024)
    bias = value_bias.reshape(1, HD)
    tp = lax.axis_index("tp")
    place = lax.axis_index(PLACE)

    own = jnp.concatenate([hidden_context, hidden_rows], axis=0)
    low = move_x(own, 1)
    high = move_x(own, -1)
    twin = swap_core(own)
    across = [move_x(low[:TOP], 1), move_x(high[TOP:], -1)]
    low_twin = swap_core(low)
    high_twin = swap_core(high)
    far = jnp.concatenate(across, axis=0)
    far_twin = swap_core(far)
    mate = tp ^ 1

    def owners(*places):
        return jnp.stack([place % 8 for place in places]).astype(jnp.int32)

    state = project([own, twin], owners(tp, mate), weights, gain, None, None)
    state = project(
        [low, high, low_twin, high_twin],
        owners(tp + 6, tp + 2, mate + 6, mate + 2),
        weights,
        gain,
        state,
        None,
    )
    pairs, row_pairs = project(
        [far, far_twin], owners(tp + 4, mate + 4), weights, gain, state, bias
    )

    above, below = pairs, pairs
    pieces = [pairs]
    for _ in range(3):
        above, below = move(above, 1, 0), move(below, -1, 0)
        pieces += [above, below]
    pieces += [move(above[: TOK // 2], 1, 0), move(below[TOK // 2 :], -1, 0)]
    line = jnp.concatenate(pieces, axis=0)
    half = line.shape[0] // 2
    line_before = move(line, 0, 1)
    line_after = move(line, 0, -1)
    line_far = [move(line_before[:half], 0, 1), move(line_after[half:], 0, -1)]

    rim = lax.ppermute(row_pairs, PLACE, [(i, i + 1) for i in range(31)])
    nodes = row_node.reshape(-1, ROW)
    own_nodes = lax.dynamic_index_in_dim(nodes, place, 0, keepdims=False)
    rim_nodes = lax.dynamic_index_in_dim(nodes, jnp.maximum(place - 1, 0), 0, keepdims=False)
    rim_nodes = jnp.where(place > 0, rim_nodes, -1)
    seats = jnp.arange(ROW, dtype=jnp.int32)
    seat_ok = jnp.concatenate(
        [
            rim_nodes[None, :] == own_nodes[:, None],
            (seats[None, :] <= seats[:, None]) & (own_nodes[None, :] == own_nodes[:, None]),
            jnp.zeros((ROW, HD - 2 * ROW), bool),
        ],
        axis=1,
    )
    extra = (
        jnp.concatenate([rim, row_pairs, jnp.zeros((HD - 2 * ROW, 2 * HD), jnp.bfloat16)], axis=0),
        jnp.repeat(seat_ok.astype(jnp.float32), GROUP, axis=0),
    )
    reach = jnp.broadcast_to(context_length[:, None, None], (ROW, GROUP, HD))
    reach = reach.reshape(ROW * GROUP, HD)
    longest = jnp.max(context_length)
    row_queries = query_rows.reshape(ROW * GROUP, HD)

    y = (place // RUN) % RING_Y
    z = (place // (RING_Y * RUN)) * RUN + place % RUN
    order = jnp.array([0, 7, 1, 6, 2, 5, 3, 4], jnp.int32)
    spots = (z + order) % RING_Z

    def info(*ys):
        groups = [jnp.stack([yy % RING_Y, RING_Y + yy % RING_Y]) for yy in ys]
        groups = jnp.concatenate(groups + [jnp.zeros((6 - 2 * len(ys),), jnp.int32)])
        return jnp.concatenate(
            [jnp.stack([place, longest]), groups] + [spots + 8 * i for i in range(len(ys))]
        ).astype(jnp.int32)

    run = functools.partial(
        stage, query=query_context, query_rows=row_queries, lengths=reach
    )
    state = run(1, info(y), [line], extra=extra, state=None, last=False)
    state = run(2, info(y + 3, y + 1), [line_before, line_after], extra=None, state=state, last=False)
    out, out_rows = run(1, info(y + 2), line_far, extra=None, state=state, last=True)
    return out, out_rows.reshape(ROW, GROUP * HD)


def solution(mesh):
    return jax.shard_map(
        per_device,
        mesh=mesh,
        in_specs=(
            P(PLACE, "tp"),
            P(PLACE, "tp"),
            P(),
            P(None, None, "tp"),
            P("tp"),
            P(PLACE, "tp"),
            P(PLACE, "tp"),
            P(PLACE),
            P(),
        ),
        out_specs=(P(PLACE, "tp"), P(PLACE, "tp")),
        check_vma=False,
    )
```

```python
import functools
import math

import jax
import jax.numpy as jnp
from jax import lax
from jax.experimental import pallas as pl
from jax.experimental.pallas import tpu as pltpu
from jax.sharding import PartitionSpec as P

D = 8192
H = 64
KVH = 8
HD = 128
STEPS = 4
GROUP = H // KVH

PLACE = ("sec", "seq")
RING_Z, RING_Y, RUN = 8, 4, 4
TOK = 256
ROW = 16
BOTH = TOK + ROW
TOP = 128
WIDE = 1024
LOWEST = -1e30
SCALE = math.log2(math.e) / math.sqrt(HD)
VMEM = 32 * 1024 * 1024
IN_VMEM = pl.BlockSpec(memory_space=pltpu.VMEM)
IN_SMEM = pl.BlockSpec(memory_space=pltpu.SMEM)


def place_of(y, z):
    return (z // RUN) * (RING_Y * RUN) + y * RUN + z % RUN


def move(block, dz, dy):
    route = [
        (place_of(y, z), place_of((y + dy) % RING_Y, (z + dz) % RING_Z))
        for y in range(RING_Y)
        for z in range(RING_Z)
    ]
    return lax.ppermute(block, PLACE, route)


def move_x(block, step):
    return lax.ppermute(block, "tp", [(i, (i + 2 * step) % 8) for i in range(8)])


def swap_core(block):
    return lax.ppermute(block, "tp", [(i, i ^ 1) for i in range(8)])


def project_kernel(count, shifts, first, last, tp_ref, *refs):
    refs = list(refs)
    pieces = [refs.pop(0) for _ in range(count)]
    weights, gain = refs.pop(0), refs.pop(0)
    if not first:
        product_in, squares_in = refs.pop(0), refs.pop(0)
    if last:
        bias = refs.pop(0)
    product = jnp.zeros((BOTH, 2 * HD), jnp.float32) if first else product_in[...]
    squares = jnp.zeros((BOTH, HD), jnp.float32) if first else squares_in[...]
    for piece, (step, other) in zip(pieces, shifts):
        tp = tp_ref[0]
        base = tp + 1 - 2 * (tp % 2) if other else tp
        owner = (base + 2 * step + 8) % 8
        own_gain = gain[pl.ds(owner, 1), :]
        for begin in range(0, WIDE, 256):
            wide = piece[:, begin : begin + 256].astype(jnp.float32)
            squared = wide * wide
            squares = squares + (squared[:, :HD] + squared[:, HD:])
            scaled = (wide * own_gain[:, begin : begin + 256]).astype(jnp.bfloat16)
            rows = pl.ds(pl.multiple_of(owner * WIDE + begin, 256), 256)
            product = product + jnp.dot(
                scaled, weights[rows, :], preferred_element_type=jnp.float32
            )
    if not last:
        refs[0][...] = product
        refs[1][...] = squares
        return
    inverse = lax.rsqrt(jnp.sum(squares, axis=1, keepdims=True) / D + 1e-06)
    keys = (product[:, :HD] * inverse).astype(jnp.bfloat16)
    values = (product[:, HD:] * inverse + bias[...]).astype(jnp.bfloat16)
    refs[0][:, :HD] = keys[:TOK]
    refs[0][:, HD:] = values[:TOK]
    refs[1][:, :HD] = keys[TOK:]
    refs[1][:, HD:] = values[TOK:]


def project(tp, pieces, shifts, weights, gain, state, bias):
    count = len(pieces)
    first, last = state is None, bias is not None
    operands = [tp] + list(pieces) + [weights, gain]
    if not first:
        operands += list(state)
    if last:
        operands.append(bias)
        shapes = [
            jax.ShapeDtypeStruct((TOK, 2 * HD), jnp.bfloat16),
            jax.ShapeDtypeStruct((ROW, 2 * HD), jnp.bfloat16),
        ]
    else:
        shapes = [
            jax.ShapeDtypeStruct((BOTH, 2 * HD), jnp.float32),
            jax.ShapeDtypeStruct((BOTH, HD), jnp.float32),
        ]
    return pl.pallas_call(
        functools.partial(project_kernel, count, shifts, first, last),
        in_specs=[IN_SMEM] + [IN_VMEM] * (len(operands) - 1),
        out_specs=[IN_VMEM] * 2,
        out_shape=shapes,
        compiler_params=pltpu.CompilerParams(vmem_limit_bytes=VMEM),
        cost_estimate=pl.CostEstimate(
            flops=count * BOTH * WIDE * 512, bytes_accessed=count * 1100000, transcendentals=0
        ),
    )(*operands)


def attend(queries, keys, values, allowed, top_ref, mixed_ref, rows):
    parts = []
    highest = None
    for number in range(len(keys)):
        scores = lax.dot_general(
            queries, keys[number], (((1,), (1,)), ((), ())), preferred_element_type=jnp.float32
        )
        scores = scores * SCALE
        if allowed is not None:
            scores = jnp.where(allowed[number], scores, LOWEST)
        parts.append(scores)
        for begin in range(0, scores.shape[1], HD):
            piece = scores[:, begin : begin + HD]
            highest = piece if highest is None else jnp.maximum(highest, piece)
    before = top_ref[rows, :]
    top = jnp.maximum(before, jnp.max(highest, axis=1, keepdims=True))
    factor = jnp.exp2(before - top)
    mixed = mixed_ref[rows, :] * jnp.concatenate([factor, factor], axis=1)
    for number in range(len(keys)):
        width = parts[number].shape[1]
        lifted = jnp.concatenate([top] * (width // HD), axis=1)
        weight = jnp.exp2(parts[number] - lifted)
        mixed = mixed + jnp.dot(
            weight.astype(jnp.bfloat16), values[number], preferred_element_type=jnp.float32
        )
    top_ref[rows, :] = top
    mixed_ref[rows, :] = mixed


def per_row(table, begin):
    seat = lax.broadcasted_iota(jnp.int32, (ROW, HD), 0)
    found = jnp.zeros((ROW, HD), jnp.int32)
    for row in range(ROW):
        found = jnp.where(seat == row, table[begin + row], found)
    return found


def stage_kernel(offsets, counts, first, last, place_ref, length_ref, *refs):
    refs = list(refs)
    node_ref = refs.pop(0) if first else None
    blocks = [refs.pop(0) for _ in counts]
    query, query_rows = refs.pop(0), refs.pop(0)
    if first:
        rim, row_pairs = refs.pop(0), refs.pop(0)
    else:
        refs = refs[2:]
    if last:
        out, out_rows = refs.pop(0), refs.pop(0)
    top_ref, mixed_ref, keys, values, listed, numbers = refs
    place = place_ref[0]
    y, z = (place // RUN) % RING_Y, (place // (RING_Y * RUN)) * RUN + place % RUN
    longest = length_ref[0]
    for row in range(1, ROW):
        longest = jnp.maximum(longest, length_ref[row])

    slot = 0
    for block, count in zip(blocks, counts):
        for number in range(count):
            held = slice(slot * TOK, (slot + 1) * TOK)
            here = slice(number * TOK, (number + 1) * TOK)
            keys[held, :] = block[here, :HD]
            values[held, :HD] = block[here, HD:]
            slot += 1
    values[:, HD:] = jnp.ones((values.shape[0], HD), jnp.bfloat16)

    full, loose = jnp.int32(0), jnp.int32(0)
    for slot, (dz, dy) in enumerate(offsets):
        far_y, far_z = (y + dy + RING_Y) % RING_Y, (z + dz + RING_Z) % RING_Z
        number = (far_z // RUN) * (RING_Y * RUN) + far_y * RUN + far_z % RUN
        numbers[slot] = number
        listed[full] = jnp.int32(slot)
        full = full + (number < place).astype(jnp.int32)
        listed[16 + loose] = jnp.int32(slot)
        loose = loose + ((number > place) & (number * TOK < longest)).astype(jnp.int32)

    lengths = per_row(length_ref, 0)
    decode_rows = slice(GROUP * TOK, GROUP * (TOK + ROW))
    decode_query = jnp.concatenate(
        [query_rows[:, head * HD : (head + 1) * HD] for head in range(GROUP)], axis=0
    )
    lane = lax.broadcasted_iota(jnp.int32, (ROW, TOK), 1)

    def decode(slots, some_keys, some_values):
        allowed = []
        for slot in slots:
            reach = lengths - numbers[slot] * TOK
            fits = lane < jnp.concatenate([reach, reach], axis=1)
            allowed.append(jnp.concatenate([fits] * GROUP, axis=0))
        attend(decode_query, some_keys, some_values, allowed, top_ref, mixed_ref, decode_rows)

    def load(slots):
        spans = [pl.ds(pl.multiple_of(slot * TOK, TOK), TOK) for slot in slots]
        return [keys[span, :] for span in spans], [values[span, :] for span in spans]

    def prefill(some_keys, some_values, allowed):
        for head in range(GROUP):
            attend(
                query[:, head * HD : (head + 1) * HD],
                some_keys,
                some_values,
                allowed,
                top_ref,
                mixed_ref,
                slice(head * TOK, (head + 1) * TOK),
            )

    if first:
        top_ref[...] = jnp.full(top_ref.shape, LOWEST, jnp.float32)
        mixed_ref[...] = jnp.zeros(mixed_ref.shape, jnp.float32)
        nodes = per_row(node_ref, place * ROW)
        seat = lax.broadcasted_iota(jnp.int32, (ROW, HD), 0)
        column = lax.broadcasted_iota(jnp.int32, (ROW, HD), 1)
        key_nodes = jnp.full((ROW, HD), -1, jnp.int32)
        previous = jnp.maximum(place - 1, 0) * ROW
        for row in range(ROW):
            rim_node = jnp.where(place > 0, node_ref[previous + row], -1)
            key_nodes = jnp.where(column == row, rim_node, key_nodes)
            key_nodes = jnp.where(column == ROW + row, node_ref[place * ROW + row], key_nodes)
        same = (key_nodes == nodes) & (column <= seat + ROW)
        pad = jnp.zeros((HD - 2 * ROW, HD), jnp.bfloat16)
        ones = jnp.ones((HD, HD), jnp.bfloat16)
        extra_keys = jnp.concatenate([rim[:, :HD], row_pairs[:, :HD], pad], axis=0)
        extra_values = jnp.concatenate([rim[:, HD:], row_pairs[:, HD:], pad], axis=0)
        attend(
            decode_query,
            [extra_keys],
            [jnp.concatenate([extra_values, ones], axis=1)],
            [jnp.concatenate([same] * GROUP, axis=0)],
            top_ref,
            mixed_ref,
            decode_rows,
        )
        token = lax.broadcasted_iota(jnp.int32, (TOK, TOK), 0)
        some_keys, some_values = [keys[:TOK, :]], [values[:TOK, :]]
        prefill(some_keys, some_values, [lax.broadcasted_iota(jnp.int32, (TOK, TOK), 1) <= token])
        decode([0], some_keys, some_values)

    def four(turn, carry):
        slots = [listed[4 * turn + i] for i in range(4)]
        some_keys, some_values = load(slots)
        prefill(some_keys, some_values, None)
        decode(slots, some_keys, some_values)
        return carry

    def one(turn, carry):
        slots = [listed[turn]]
        some_keys, some_values = load(slots)
        prefill(some_keys, some_values, None)
        decode(slots, some_keys, some_values)
        return carry

    def rows_only(turn, carry):
        slots = [listed[16 + turn]]
        decode(slots, *load(slots))
        return carry

    lax.fori_loop(0, full // 4, four, 0)
    lax.fori_loop((full // 4) * 4, full, one, 0)
    lax.fori_loop(0, loose, rows_only, 0)

    if last:
        for head in range(GROUP):
            mixed = mixed_ref[head * TOK : (head + 1) * TOK, :]
            result = mixed[:, :HD] / mixed[:, HD:]
            out[:, head * HD : (head + 1) * HD] = result.astype(out.dtype)
            begin = GROUP * TOK + head * ROW
            mixed = mixed_ref[begin : begin + ROW, :]
            result = mixed[:, :HD] / mixed[:, HD:]
            out_rows[:, head * HD : (head + 1) * HD] = result.astype(out.dtype)


def stage(place, lengths, nodes, blocks, offsets, query, query_rows, rows, state, last):
    first = state is None
    counts = [block.shape[0] // TOK for block in blocks]
    total = sum(counts)
    smem = [place, lengths] + ([nodes] if first else [])
    operands = smem + list(blocks) + [query, query_rows] + list(rows if first else state)
    height = GROUP * (TOK + ROW)
    state_shapes = [
        jax.ShapeDtypeStruct((height, HD), jnp.float32),
        jax.ShapeDtypeStruct((height, 2 * HD), jnp.float32),
    ]
    scratch = [
        pltpu.VMEM((total * TOK, HD), jnp.bfloat16),
        pltpu.VMEM((total * TOK, 2 * HD), jnp.bfloat16),
        pltpu.SMEM((32,), jnp.int32),
        pltpu.SMEM((16,), jnp.int32),
    ]
    out_shapes = [
        jax.ShapeDtypeStruct(query.shape, jnp.bfloat16),
        jax.ShapeDtypeStruct(query_rows.shape, jnp.bfloat16),
    ]
    shapes = (out_shapes if last else []) + state_shapes
    begin = len(operands) - 2
    aliases = {} if first else {begin + i: len(shapes) - 2 + i for i in range(2)}
    work = total * TOK * TOK * GROUP
    results = pl.pallas_call(
        functools.partial(stage_kernel, offsets, counts, first, last),
        in_specs=[IN_SMEM] * len(smem) + [IN_VMEM] * (len(operands) - len(smem)),
        out_specs=[IN_VMEM] * len(shapes),
        out_shape=shapes,
        scratch_shapes=scratch,
        input_output_aliases=aliases,
        compiler_params=pltpu.CompilerParams(vmem_limit_bytes=VMEM),
        cost_estimate=pl.CostEstimate(
            flops=work * 8 * HD, bytes_accessed=2000000, transcendentals=work
        ),
    )(*operands)
    return results[:2]


def per_device(
    hidden_context,
    hidden_rows,
    norm_gain,
    key_value_weight,
    value_bias,
    query_context,
    query_rows,
    context_length,
    row_node,
):
    weights = key_value_weight.reshape(D, 2 * HD)
    gain = norm_gain.reshape(8, WIDE)
    bias = value_bias.reshape(1, HD)
    tp = lax.axis_index("tp").astype(jnp.int32).reshape(1)
    place = lax.axis_index(PLACE).astype(jnp.int32).reshape(1)

    own = jnp.concatenate([hidden_context, hidden_rows], axis=0)
    low, high, twin = move_x(own, 1), move_x(own, -1), swap_core(own)
    add = functools.partial(project, tp, weights=weights, gain=gain)
    state = add([own, twin], [(0, 0), (0, 1)], state=None, bias=None)
    low, high, state = lax.optimization_barrier((low, high, state))
    far_low, far_high = move_x(low[:TOP], 1), move_x(high[TOP:], -1)
    low_twin, high_twin = swap_core(low), swap_core(high)
    state = add(
        [low, high, low_twin, high_twin],
        [(-1, 0), (1, 0), (-1, 1), (1, 1)],
        state=state,
        bias=None,
    )
    far_low, far_high, state = lax.optimization_barrier((far_low, far_high, state))
    far = jnp.concatenate([far_low, far_high], axis=0)
    far_twin = swap_core(far)
    state = add([far], [(2, 0)], state=state, bias=None)
    pairs, row_pairs = add([far_twin], [(2, 1)], state=state, bias=bias)

    above, below = [pairs], [pairs]
    for _ in range(3):
        above.append(move(above[-1], 1, 0))
        below.append(move(below[-1], -1, 0))
    ends = [move(above[3][:TOP], 1, 0), move(below[3][TOP:], -1, 0)]
    rim = lax.ppermute(row_pairs, PLACE, [(i, i + 1) for i in range(31)])

    near = jnp.concatenate([pairs, above[1], below[1], above[2], below[2]], axis=0)
    wide = jnp.concatenate([above[3], below[3]] + ends, axis=0)
    near_steps, wide_steps = [0, -1, 1, -2, 2], [-3, 3, 4]
    near_up, near_down = move(near, 0, 1), move(near, 0, -1)
    wide_up, wide_down = move(wide, 0, 1), move(wide, 0, -1)
    cut = 3 * TOK
    near_far = [move(near_up[:cut], 0, 1), move(near_down[cut:], 0, -1)]
    cut = 1 * TOK
    wide_far = [move(wide_up[:cut], 0, 1), move(wide_down[cut:], 0, -1)]

    def at(steps, dy):
        return [(step, dy) for step in steps]

    run = functools.partial(
        stage, place, context_length, row_node, query=query_context, query_rows=query_rows
    )
    state = run([near], at(near_steps, 0), rows=[rim, row_pairs], state=None, last=False)
    state = run(
        [wide, near_up, near_down],
        at(wide_steps, 0) + at(near_steps, -1) + at(near_steps, 1),
        rows=None,
        state=state,
        last=False,
    )
    state = run(
        [wide_up, wide_down] + near_far,
        at(wide_steps, -1) + at(wide_steps, 1) + at(near_steps, 2),
        rows=None,
        state=state,
        last=False,
    )
    out, out_rows = run(wide_far, at(wide_steps, 2), rows=None, state=state, last=True)
    return out, out_rows


def solution(mesh):
    return jax.shard_map(
        per_device,
        mesh=mesh,
        in_specs=(
            P(PLACE, "tp"),
            P(PLACE, "tp"),
            P(),
            P(None, None, "tp"),
            P("tp"),
            P(PLACE, "tp"),
            P(PLACE, "tp"),
            P(PLACE),
            P(),
        ),
        out_specs=(P(PLACE, "tp"), P(PLACE, "tp")),
        check_vma=False,
    )
```

```python
import functools
import math

import jax
import jax.numpy as jnp
from jax import lax
from jax.experimental import pallas as pl
from jax.experimental.pallas import tpu as pltpu
from jax.sharding import PartitionSpec as P

D = 8192
H = 64
KVH = 8
HD = 128
STEPS = 4
GROUP = H // KVH

PLACE = ("sec", "seq")
RING_Z, RING_Y, RUN = 8, 4, 4
TOK = 256
ROW = 16
BOTH = TOK + ROW
TOP = 128
WIDE = 1024
HEIGHT = GROUP * (TOK + ROW)
LEVELS = 32
LOWEST = -1e30
SCALE = math.log2(math.e) / math.sqrt(HD)
VMEM = 32 * 1024 * 1024
IN_VMEM = pl.BlockSpec(memory_space=pltpu.VMEM)
IN_SMEM = pl.BlockSpec(memory_space=pltpu.SMEM)
IN_HBM = pl.BlockSpec(memory_space=pltpu.HBM)


def place_of(y, z):
    return (z // RUN) * (RING_Y * RUN) + y * RUN + z % RUN


def move(block, dz, dy):
    route = [
        (place_of(y, z), place_of((y + dy) % RING_Y, (z + dz) % RING_Z))
        for y in range(RING_Y)
        for z in range(RING_Z)
    ]
    return lax.ppermute(block, PLACE, route)


def move_x(block, step):
    return lax.ppermute(block, "tp", [(i, (i + 2 * step) % 8) for i in range(8)])


def swap_core(block):
    return lax.ppermute(block, "tp", [(i, i ^ 1) for i in range(8)])


def project_kernel(count, shifts, first, last, tp_ref, *refs):
    refs = list(refs)
    pieces = [[refs.pop(0) for _ in range(parts)] for parts in count]
    weights, gain = refs.pop(0), refs.pop(0)
    if not first:
        product_in, squares_in = refs.pop(0), refs.pop(0)
    if last:
        bias = refs.pop(0)
    ready, held = refs.pop(), refs.pop()
    tp = tp_ref[0]
    mate = tp + 1 - 2 * (tp % 2)
    owners = [((mate if other else tp) + 2 * step + 8) % 8 for step, other in shifts]
    copies = []
    for number, owner in enumerate(owners):
        rows = pl.ds(pl.multiple_of(owner * WIDE, WIDE), WIDE)
        copies.append(
            pltpu.make_async_copy(weights.at[rows, :], held.at[number], ready.at[number])
        )
        copies[-1].start()
    product = jnp.zeros((BOTH, 2 * HD), jnp.float32) if first else product_in[...]
    squares = jnp.zeros((BOTH, HD), jnp.float32) if first else squares_in[...]
    for number, (piece, owner) in enumerate(zip(pieces, owners)):
        copies[number].wait()
        own_gain = gain[pl.ds(owner, 1), :]
        for begin in range(0, WIDE, 256):
            chunks = [chunk[:, begin : begin + 256] for chunk in piece]
            wide = jnp.concatenate(chunks, axis=0).astype(jnp.float32)
            squared = wide * wide
            squares = squares + (squared[:, :HD] + squared[:, HD:])
            scaled = (wide * own_gain[:, begin : begin + 256]).astype(jnp.bfloat16)
            product = product + jnp.dot(
                scaled, held[number, begin : begin + 256, :], preferred_element_type=jnp.float32
            )
    if not last:
        refs[0][...] = product
        refs[1][...] = squares
        return
    inverse = lax.rsqrt(jnp.sum(squares, axis=1, keepdims=True) / D + 1e-06)
    keys = (product[:, :HD] * inverse).astype(jnp.bfloat16)
    values = (product[:, HD:] * inverse + bias[...]).astype(jnp.bfloat16)
    refs[0][:, :HD] = keys[:TOK]
    refs[0][:, HD:] = values[:TOK]
    refs[1][:, :HD] = keys[TOK:]
    refs[1][:, HD:] = values[TOK:]


def project(tp, pieces, shifts, weights, gain, state, bias):
    count = [len(piece) for piece in pieces]
    first, last = state is None, bias is not None
    operands = [tp] + [chunk for piece in pieces for chunk in piece] + [weights, gain]
    specs = [IN_SMEM] + [IN_VMEM] * sum(count) + [IN_HBM, IN_VMEM]
    if not first:
        operands += list(state)
    if last:
        operands.append(bias)
        shapes = [
            jax.ShapeDtypeStruct((TOK, 2 * HD), jnp.bfloat16),
            jax.ShapeDtypeStruct((ROW, 2 * HD), jnp.bfloat16),
        ]
    else:
        shapes = [
            jax.ShapeDtypeStruct((BOTH, 2 * HD), jnp.float32),
            jax.ShapeDtypeStruct((BOTH, HD), jnp.float32),
        ]
    specs += [IN_VMEM] * (len(operands) - len(specs))
    return pl.pallas_call(
        functools.partial(project_kernel, count, shifts, first, last),
        in_specs=specs,
        out_specs=[IN_VMEM] * 2,
        out_shape=shapes,
        scratch_shapes=[
            pltpu.VMEM((len(count), WIDE, 2 * HD), jnp.bfloat16),
            pltpu.SemaphoreType.DMA((len(count),)),
        ],
        compiler_params=pltpu.CompilerParams(vmem_limit_bytes=VMEM),
        cost_estimate=pl.CostEstimate(
            flops=len(count) * BOTH * WIDE * 512,
            bytes_accessed=len(count) * 1100000,
            transcendentals=0,
        ),
    )(*operands)


def attend(queries, keys, values, allowed, guard, top_ref, mixed_ref, rows):
    parts = []
    highest = None
    for number in range(len(keys)):
        scores = lax.dot_general(
            queries, keys[number], (((1,), (1,)), ((), ())), preferred_element_type=jnp.float32
        )
        scores = scores * SCALE
        if allowed is not None:
            scores = jnp.where(allowed[number], scores, LOWEST)
        parts.append(scores)
        for begin in range(0, scores.shape[1], HD):
            piece = scores[:, begin : begin + HD]
            highest = piece if highest is None else jnp.maximum(highest, piece)
    before = top_ref[rows, :]
    top = jnp.maximum(before, jnp.max(highest, axis=1, keepdims=True))
    factor = jnp.exp2(before - top)
    mixed = mixed_ref[rows, :] * jnp.concatenate([factor, factor], axis=1)
    for number in range(len(keys)):
        width = parts[number].shape[1]
        lifted = jnp.concatenate([top] * (width // HD), axis=1)
        weight = jnp.exp2(parts[number] - lifted)
        if guard:
            weight = jnp.where(allowed[number], weight, 0.0)
        mixed = mixed + jnp.dot(
            weight.astype(jnp.bfloat16), values[number], preferred_element_type=jnp.float32
        )
    top_ref[rows, :] = top
    mixed_ref[rows, :] = mixed


def per_row(table, begin):
    seat = lax.broadcasted_iota(jnp.int32, (ROW, HD), 0)
    found = jnp.zeros((ROW, HD), jnp.int32)
    for row in range(ROW):
        found = jnp.where(seat == row, table[begin + row], found)
    return found


def head_rows(pack):
    rows = pack[TOK : TOK + ROW, :]
    return [rows[:, head * HD : (head + 1) * HD] for head in range(GROUP)]


def reach_of(pack):
    coded = pack[TOK + ROW :, : 2 * HD].astype(jnp.float32)
    return coded[:, :HD] * 64.0 + coded[:, HD:]


def diagonal():
    row = lax.broadcasted_iota(jnp.int32, (HD, HD), 0)
    return row == lax.broadcasted_iota(jnp.int32, (HD, HD), 1)


def seal(top_ref, mixed_ref, begin, count, to, packed, levels):
    rows = slice(begin, begin + count)
    mixed = mixed_ref[rows, :]
    amount = mixed[:, HD:]
    some = amount > 0.0
    safe = jnp.where(some, amount, 1.0)
    packed[to : to + count, :] = (mixed[:, :HD] / safe).astype(jnp.bfloat16)
    level = jnp.where(some, top_ref[rows, :] + jnp.log2(safe), LOWEST)
    seat = lax.broadcasted_iota(jnp.int32, levels.shape, 0)
    for start in range(0, count, HD):
        flat = jnp.sum(
            jnp.where(diagonal(), level[start : start + HD, :], 0.0), axis=0, keepdims=True
        )
        levels = jnp.where(seat == (to + start) // HD, flat, levels)
    return levels


def stage_kernel(plan, place_ref, *refs):
    refs = list(refs)
    init, finish, extra = plan["init"], plan["finish"], plan["extra"]
    own, mate, carrier = plan["own"], plan["mate"], plan["carrier"]
    rows_too = carrier is not None or extra
    node_ref = refs.pop(0) if extra else None
    blocks = [refs.pop(0) for _ in plan["counts"]]
    own_pack, mate_pack = refs.pop(0), refs.pop(0)
    if extra:
        rim, row_pairs = refs.pop(0), refs.pop(0)
    if not init:
        refs = refs[2 * (own + mate + rows_too) :]
    packed = refs.pop(0) if finish else None
    if own:
        own_top, own_mixed = refs.pop(0), refs.pop(0)
    if mate:
        mate_top, mate_mixed = refs.pop(0), refs.pop(0)
    if rows_too:
        rows_top, rows_mixed = refs.pop(0), refs.pop(0)
    keys, values, own_list, mate_list, loose_list, numbers = refs
    place = place_ref[0]
    mate_place = place + RUN - 2 * RUN * ((place // RUN) % 2)
    y, z = (place // RUN) % RING_Y, (place // (RING_Y * RUN)) * RUN + place % RUN

    slot = 0
    for block, count in zip(blocks, plan["counts"]):
        for number in range(count):
            held = slice(slot * TOK, (slot + 1) * TOK)
            here = slice(number * TOK, (number + 1) * TOK)
            keys[held, :] = block[here, :HD]
            values[held, :HD] = block[here, HD:]
            slot += 1
    values[:, HD:] = jnp.ones((values.shape[0], HD), jnp.bfloat16)

    if rows_too:
        decode_query = jnp.concatenate(head_rows(own_pack) + head_rows(mate_pack), axis=0)
    if carrier is not None:
        own_reach, mate_reach = reach_of(own_pack), reach_of(mate_pack)
        longest = jnp.max(jnp.maximum(own_reach, mate_reach))
        lane = lax.broadcasted_iota(jnp.int32, (ROW, TOK), 1).astype(jnp.float32)

    own_count, mate_count, loose_count = jnp.int32(0), jnp.int32(0), jnp.int32(0)
    for slot, (dz, other) in enumerate(plan["offsets"]):
        far_y, far_z = (RING_Y - 1 - y) if other else y, (z + dz + RING_Z) % RING_Z
        number = (far_z // RUN) * (RING_Y * RUN) + far_y * RUN + far_z % RUN
        numbers[slot] = number
        own_list[own_count] = jnp.int32(slot)
        own_count = own_count + (number < place).astype(jnp.int32)
        mate_list[mate_count] = jnp.int32(slot)
        mate_count = mate_count + (number < mate_place).astype(jnp.int32)
        if carrier is not None:
            bound = mate_place if carrier == "mate" else place
            left = (number >= bound) & ((number * TOK).astype(jnp.float32) < longest)
            loose_list[loose_count] = jnp.int32(slot)
            loose_count = loose_count + left.astype(jnp.int32)

    def load(slots):
        spans = [pl.ds(pl.multiple_of(slot * TOK, TOK), TOK) for slot in slots]
        return [keys[span, :] for span in spans], [values[span, :] for span in spans]

    def decode(slots, some_keys, some_values):
        allowed = []
        for slot in slots:
            base = (numbers[slot] * TOK).astype(jnp.float32)
            fits = []
            for reach in (own_reach, mate_reach):
                left = reach - base
                fits += [lane < jnp.concatenate([left, left], axis=1)] * GROUP
            allowed.append(jnp.concatenate(fits, axis=0))
        attend(
            decode_query,
            some_keys,
            some_values,
            allowed,
            True,
            rows_top,
            rows_mixed,
            slice(0, 2 * GROUP * ROW),
        )

    def prefill(pack, some_keys, some_values, allowed, top_ref, mixed_ref):
        for head in range(GROUP):
            attend(
                pack[:TOK, head * HD : (head + 1) * HD],
                some_keys,
                some_values,
                allowed,
                False,
                top_ref,
                mixed_ref,
                slice(head * TOK, (head + 1) * TOK),
            )

    if init:
        for top_ref, mixed_ref in (
            (own_top, own_mixed),
            (mate_top, mate_mixed),
            (rows_top, rows_mixed),
        ):
            top_ref[...] = jnp.full(top_ref.shape, LOWEST, jnp.float32)
            mixed_ref[...] = jnp.zeros(mixed_ref.shape, jnp.float32)
        token = lax.broadcasted_iota(jnp.int32, (TOK, TOK), 0)
        causal = [lax.broadcasted_iota(jnp.int32, (TOK, TOK), 1) <= token]
        some_keys, some_values = [keys[:TOK, :]], [values[:TOK, :]]
        prefill(own_pack, some_keys, some_values, causal, own_top, own_mixed)
        decode([0], some_keys, some_values)

    def sweep(pack, listed, count, top_ref, mixed_ref, with_rows):
        def turn_of(size):
            def turn(number, carry):
                slots = [listed[size * number + i] for i in range(size)]
                some_keys, some_values = load(slots)
                prefill(pack, some_keys, some_values, None, top_ref, mixed_ref)
                if with_rows:
                    decode(slots, some_keys, some_values)
                return carry

            return turn

        if len(plan["offsets"]) > 3:
            lax.fori_loop(0, count // 4, turn_of(4), 0)
        lax.fori_loop((count // 4) * 4, count, turn_of(1), 0)

    if own and not init:
        sweep(own_pack, own_list, own_count, own_top, own_mixed, carrier == "own")
    if mate:
        sweep(mate_pack, mate_list, mate_count, mate_top, mate_mixed, carrier == "mate")
    if carrier is not None and not init:

        def rows_only(turn, carry):
            slots = [loose_list[turn]]
            decode(slots, *load(slots))
            return carry

        lax.fori_loop(0, loose_count, rows_only, 0)

    if extra:
        nodes = per_row(node_ref, place * ROW)
        seat = lax.broadcasted_iota(jnp.int32, (ROW, HD), 0)
        column = lax.broadcasted_iota(jnp.int32, (ROW, HD), 1)
        key_nodes = jnp.full((ROW, HD), -1, jnp.int32)
        previous = jnp.maximum(place - 1, 0) * ROW
        for row in range(ROW):
            rim_node = jnp.where(place > 0, node_ref[previous + row], -1)
            key_nodes = jnp.where(column == row, rim_node, key_nodes)
            key_nodes = jnp.where(column == ROW + row, node_ref[place * ROW + row], key_nodes)
        same = (key_nodes == nodes) & (column <= seat + ROW)
        pad = jnp.zeros((HD - 2 * ROW, HD), jnp.bfloat16)
        ones = jnp.ones((HD, HD), jnp.bfloat16)
        extra_keys = jnp.concatenate([rim[:, :HD], row_pairs[:, :HD], pad], axis=0)
        extra_values = jnp.concatenate([rim[:, HD:], row_pairs[:, HD:], pad], axis=0)
        attend(
            decode_query[: GROUP * ROW],
            [extra_keys],
            [jnp.concatenate([extra_values, ones], axis=1)],
            [jnp.concatenate([same] * GROUP, axis=0)],
            True,
            rows_top,
            rows_mixed,
            slice(0, GROUP * ROW),
        )

    if finish:
        levels = jnp.zeros((LEVELS, HD), jnp.float32)
        for head in range(GROUP):
            levels = seal(mate_top, mate_mixed, head * TOK, TOK, head * TOK, packed, levels)
        levels = seal(rows_top, rows_mixed, GROUP * ROW, HD, GROUP * TOK, packed, levels)
        for part in range(3):
            rounded = levels.astype(jnp.bfloat16)
            begin = HEIGHT + part * LEVELS
            packed[begin : begin + LEVELS, :] = rounded
            levels = levels - rounded.astype(jnp.float32)


def stage(
    place,
    packs,
    blocks,
    offsets,
    state,
    own=False,
    mate=False,
    carrier=None,
    finish=False,
    extra=None,
):
    init = state is None
    rows_too = carrier is not None or extra is not None
    plan = dict(
        counts=[block.shape[0] // TOK for block in blocks],
        offsets=offsets,
        init=init,
        own=own,
        mate=mate,
        carrier=carrier,
        finish=finish,
        extra=extra is not None,
    )
    total = len(offsets)
    smem = [place] + ([extra[0]] if extra else [])
    operands = smem + list(blocks) + list(packs) + (list(extra[1:]) if extra else [])
    used = [name for name, flag in (("own", own), ("mate", mate), ("rows", rows_too)) if flag]
    sizes = dict(own=GROUP * TOK, mate=GROUP * TOK, rows=2 * GROUP * ROW)
    shapes = [jax.ShapeDtypeStruct((HEIGHT + 3 * LEVELS, HD), jnp.bfloat16)] if finish else []
    aliases = {}
    for name in used:
        for index, width in enumerate((HD, 2 * HD)):
            if not init:
                aliases[len(operands)] = len(shapes)
                operands.append(state[name][index])
            shapes.append(jax.ShapeDtypeStruct((sizes[name], width), jnp.float32))
    work = total * TOK * TOK * GROUP * (own + mate)
    results = pl.pallas_call(
        functools.partial(stage_kernel, plan),
        in_specs=[IN_SMEM] * len(smem) + [IN_VMEM] * (len(operands) - len(smem)),
        out_specs=[IN_VMEM] * len(shapes),
        out_shape=shapes,
        scratch_shapes=[
            pltpu.VMEM((total * TOK, HD), jnp.bfloat16),
            pltpu.VMEM((total * TOK, 2 * HD), jnp.bfloat16),
        ]
        + [pltpu.SMEM((16,), jnp.int32) for _ in range(4)],
        input_output_aliases=aliases,
        compiler_params=pltpu.CompilerParams(vmem_limit_bytes=VMEM),
        cost_estimate=pl.CostEstimate(
            flops=work * 8 * HD, bytes_accessed=2000000, transcendentals=work
        ),
    )(*operands)
    results = list(results)
    packed = results.pop(0) if finish else None
    state = dict(state or {})
    for name in used:
        state[name] = (results.pop(0), results.pop(0))
    return (state, packed) if finish else state


def merge_kernel(own_top, own_mixed, rows_top, rows_mixed, packed, out, out_rows):
    levels = jnp.zeros((LEVELS, HD), jnp.float32)
    for part in range(3):
        begin = HEIGHT + part * LEVELS
        levels = levels + packed[begin : begin + LEVELS, :].astype(jnp.float32)

    def joined(top_ref, mixed_ref, begin, at):
        rows = slice(begin, begin + HD)
        flat = levels[at // HD : at // HD + 1, :]
        level = jnp.sum(jnp.where(diagonal(), flat, 0.0), axis=1, keepdims=True)
        top = top_ref[rows, :]
        highest = jnp.maximum(top, level)
        mine, theirs = jnp.exp2(top - highest), jnp.exp2(level - highest)
        mixed = mixed_ref[rows, :]
        other = packed[at : at + HD, :].astype(jnp.float32)
        amount = mine * mixed[:, HD:] + theirs
        return ((mine * mixed[:, :HD] + theirs * other) / amount).astype(jnp.bfloat16)

    for head in range(GROUP):
        for start in range(0, TOK, HD):
            begin = head * TOK + start
            part = joined(own_top, own_mixed, begin, begin)
            out[start : start + HD, head * HD : (head + 1) * HD] = part
    part = joined(rows_top, rows_mixed, 0, GROUP * TOK)
    for head in range(GROUP):
        out_rows[head] = part[head * ROW : (head + 1) * ROW, :]


def merge(state, packed):
    return pl.pallas_call(
        merge_kernel,
        in_specs=[IN_VMEM] * 5,
        out_specs=[IN_VMEM] * 2,
        out_shape=[
            jax.ShapeDtypeStruct((TOK, GROUP * HD), jnp.bfloat16),
            jax.ShapeDtypeStruct((GROUP, ROW, HD), jnp.bfloat16),
        ],
        compiler_params=pltpu.CompilerParams(vmem_limit_bytes=VMEM),
    )(*state["own"], *state["rows"], packed)


def per_device(
    hidden_context,
    hidden_rows,
    norm_gain,
    key_value_weight,
    value_bias,
    query_context,
    query_rows,
    context_length,
    row_node,
):
    weights = key_value_weight.reshape(D, 2 * HD)
    gain = norm_gain.reshape(8, WIDE)
    bias = value_bias.reshape(1, HD)
    tp = lax.axis_index("tp").astype(jnp.int32).reshape(1)
    place = lax.axis_index(PLACE).astype(jnp.int32).reshape(1)

    def swap(block, bits):
        return lax.ppermute(block, PLACE, [(i, i ^ bits) for i in range(32)])

    own = jnp.concatenate([hidden_context, hidden_rows], axis=0)
    low, high, twin = move_x(own, 1), move_x(own, -1), swap_core(own)
    digits = jnp.stack([context_length // 64, context_length % 64], axis=1)
    coded = jnp.repeat(digits.astype(jnp.bfloat16), HD, axis=1)
    coded = jnp.pad(coded, ((0, 0), (0, WIDE - 2 * HD)))
    own_pack = jnp.concatenate([query_context, query_rows, coded], axis=0)
    add = functools.partial(project, tp, weights=weights, gain=gain)
    state = add([[hidden_context, hidden_rows], [twin]], [(0, 0), (0, 1)], state=None, bias=None)
    mate_pack = swap(own_pack, RUN)
    low, high, state = lax.optimization_barrier((low, high, state))
    far_low, far_high = move_x(low[:TOP], 1), move_x(high[TOP:], -1)
    low_twin, high_twin = swap_core(low), swap_core(high)
    state = add(
        [[low], [high], [low_twin], [high_twin]],
        [(-1, 0), (1, 0), (-1, 1), (1, 1)],
        state=state,
        bias=None,
    )
    far_low, far_high, state = lax.optimization_barrier((far_low, far_high, state))
    far = jnp.concatenate([far_low, far_high], axis=0)
    far_twin = swap_core(far)
    state = add([[far_low, far_high]], [(2, 0)], state=state, bias=None)
    pairs, row_pairs = add([[far_twin]], [(2, 1)], state=state, bias=bias)

    opposite = 3 * RUN
    run = functools.partial(stage, place, (own_pack, mate_pack))
    rim = lax.ppermute(row_pairs, PLACE, [(i, i + 1) for i in range(31)])
    above, below = move(pairs, 1, 0), move(pairs, -1, 0)
    state = run([pairs], [(0, 0)], None, own=True, mate=True, carrier="own")
    above, below, state = lax.optimization_barrier((above, below, state))
    above_two, below_two = move(above, 1, 0), move(below, -1, 0)
    first = swap(jnp.concatenate([pairs, above, below], axis=0), opposite)
    above_three, below_three = move(above_two, 1, 0), move(below_two, -1, 0)
    second = swap(jnp.concatenate([above_two, below_two], axis=0), opposite)
    line = [above, below, above_two, below_two]
    steps = [(-1, 0), (1, 0), (-2, 0), (2, 0)]
    state = run(line, steps, state, own=True, carrier="own")
    above_three, below_three, state, rim = lax.optimization_barrier(
        (above_three, below_three, state, rim)
    )
    ends = [move(above_three[:TOP], 1, 0), move(below_three[TOP:], -1, 0)]
    third = swap(jnp.concatenate([above_three, below_three], axis=0), opposite)
    state = run(line, steps, state, mate=True)
    ends, state = lax.optimization_barrier((ends, state))
    end = jnp.concatenate(ends, axis=0)
    fourth = swap(end, opposite)
    line = [above_three, below_three, end, first, second]
    steps = [(-3, 0), (3, 0), (4, 0), (0, 1), (-1, 1), (1, 1), (-2, 1), (2, 1)]
    late = [third, fourth]
    late_steps = [(-3, 1), (3, 1), (4, 1)]
    state = run(line, steps, state, mate=True, carrier="mate")
    state, packed = run(late, late_steps, state, mate=True, carrier="mate", finish=True)
    sent = swap(packed, RUN)
    packed, state = lax.optimization_barrier((packed, state))
    state = run(line, steps, state, own=True)
    state = run(late, late_steps, state, own=True, extra=(row_node, rim, row_pairs))
    out, out_rows = merge(state, sent)
    return out, jnp.transpose(out_rows, (1, 0, 2)).reshape(ROW, GROUP * HD)


def solution(mesh):
    return jax.shard_map(
        per_device,
        mesh=mesh,
        in_specs=(
            P(PLACE, "tp"),
            P(PLACE, "tp"),
            P(),
            P(None, None, "tp"),
            P("tp"),
            P(PLACE, "tp"),
            P(PLACE, "tp"),
            P(PLACE),
            P(),
        ),
        out_specs=(P(PLACE, "tp"), P(PLACE, "tp")),
        check_vma=False,
    )
```

```python
import functools
import math

import jax
import jax.numpy as jnp
from jax import lax
from jax.experimental import pallas as pl
from jax.experimental.pallas import tpu as pltpu
from jax.sharding import PartitionSpec as P

D = 8192
H = 64
KVH = 8
HD = 128
STEPS = 4
GROUP = H // KVH

PLACE = ("sec", "seq")
RING_Z, RING_Y, RUN = 8, 4, 4
TOK = 256
ROW = 16
BOTH = TOK + ROW
TOP = 128
WIDE = 1024
HEIGHT = GROUP * (TOK + ROW)
LEVELS = 32
LOWEST = -1e30
SCALE = math.log2(math.e) / math.sqrt(HD)
VMEM = 32 * 1024 * 1024
IN_VMEM = pl.BlockSpec(memory_space=pltpu.VMEM)
IN_SMEM = pl.BlockSpec(memory_space=pltpu.SMEM)
IN_HBM = pl.BlockSpec(memory_space=pltpu.HBM)


def place_of(y, z):
    return (z // RUN) * (RING_Y * RUN) + y * RUN + z % RUN


def move(block, dz, dy):
    route = [
        (place_of(y, z), place_of((y + dy) % RING_Y, (z + dz) % RING_Z))
        for y in range(RING_Y)
        for z in range(RING_Z)
    ]
    return lax.ppermute(block, PLACE, route)


def move_x(block, step):
    return lax.ppermute(block, "tp", [(i, (i + 2 * step) % 8) for i in range(8)])


def swap_core(block):
    return lax.ppermute(block, "tp", [(i, i ^ 1) for i in range(8)])


def project_kernel(spans, shifts, later, held, first, last, tp_ref, *refs):
    refs = list(refs)
    pieces = [[(refs.pop(0), *span) for span in piece] for piece in spans]
    weights, gain = refs.pop(0), refs.pop(0)
    if not first:
        product_in, squares_in = refs.pop(0), refs.pop(0)
    if last:
        bias = refs.pop(0)
    tp = tp_ref[0]
    mate = tp + 1 - 2 * (tp % 2)

    def owner_of(shift):
        step, other = shift
        return ((mate if other else tp) + 2 * step + 8) % 8

    copies = []
    if held is None:
        ready, slices = refs.pop(), refs.pop()
        for number, shift in enumerate(shifts + later):
            rows = pl.ds(pl.multiple_of(owner_of(shift) * WIDE, WIDE), WIDE)
            far = number - len(shifts)
            to = slices.at[number] if far < 0 else refs[2].at[far]
            copies.append(pltpu.make_async_copy(weights.at[rows, :], to, ready.at[number]))
            copies[-1].start()
    else:
        slices = weights
    product = jnp.zeros((BOTH, 2 * HD), jnp.float32) if first else product_in[...]
    squares = jnp.zeros((BOTH, HD), jnp.float32) if first else squares_in[...]
    for number, (piece, shift) in enumerate(zip(pieces, shifts)):
        if held is None:
            copies[number].wait()
        slot = number if held is None else held[number]
        own_gain = gain[pl.ds(owner_of(shift), 1), :]
        for begin in range(0, WIDE, 256):
            chunks = [ref[start:stop, begin : begin + 256] for ref, start, stop in piece]
            wide = jnp.concatenate(chunks, axis=0).astype(jnp.float32)
            squared = wide * wide
            squares = squares + (squared[:, :HD] + squared[:, HD:])
            scaled = (wide * own_gain[:, begin : begin + 256]).astype(jnp.bfloat16)
            product = product + jnp.dot(
                scaled, slices[slot, begin : begin + 256, :], preferred_element_type=jnp.float32
            )
    for copy in copies[len(shifts) :]:
        copy.wait()
    if not last:
        refs[0][...] = product
        refs[1][...] = squares
        return
    inverse = lax.rsqrt(jnp.sum(squares, axis=1, keepdims=True) / D + 1e-06)
    keys = (product[:, :HD] * inverse).astype(jnp.bfloat16)
    values = (product[:, HD:] * inverse + bias[...]).astype(jnp.bfloat16)
    refs[0][:, :HD] = keys[:TOK]
    refs[0][:, HD:] = values[:TOK]
    refs[1][:, :HD] = keys[TOK:]
    refs[1][:, HD:] = values[TOK:]


def project(tp, gain, pieces, shifts, weights, later=(), held=None, state=None, bias=None):
    spans = [[(start, stop) for _, start, stop in piece] for piece in pieces]
    count, later = len(pieces), list(later)
    first, last = state is None, bias is not None
    operands = [tp] + [chunk[0] for piece in pieces for chunk in piece] + [weights, gain]
    specs = [IN_SMEM] + [IN_VMEM] * (len(operands) - 3)
    specs += [IN_HBM if held is None else IN_VMEM, IN_VMEM]
    if not first:
        operands += list(state)
    if last:
        operands.append(bias)
        shapes = [
            jax.ShapeDtypeStruct((TOK, 2 * HD), jnp.bfloat16),
            jax.ShapeDtypeStruct((ROW, 2 * HD), jnp.bfloat16),
        ]
    else:
        shapes = [
            jax.ShapeDtypeStruct((BOTH, 2 * HD), jnp.float32),
            jax.ShapeDtypeStruct((BOTH, HD), jnp.float32),
        ]
    if later:
        shapes.append(jax.ShapeDtypeStruct((len(later), WIDE, 2 * HD), jnp.bfloat16))
    scratch = []
    if held is None:
        scratch = [
            pltpu.VMEM((count, WIDE, 2 * HD), jnp.bfloat16),
            pltpu.SemaphoreType.DMA((count + len(later),)),
        ]
    specs += [IN_VMEM] * (len(operands) - len(specs))
    results = pl.pallas_call(
        functools.partial(project_kernel, spans, shifts, later, held, first, last),
        in_specs=specs,
        out_specs=[IN_VMEM] * len(shapes),
        out_shape=shapes,
        scratch_shapes=scratch,
        compiler_params=pltpu.CompilerParams(vmem_limit_bytes=VMEM),
        cost_estimate=pl.CostEstimate(
            flops=count * BOTH * WIDE * 512,
            bytes_accessed=count * 1100000,
            transcendentals=0,
        ),
    )(*operands)
    return (tuple(results[:2]), results[2]) if later else tuple(results)


def attend(queries, keys, values, allowed, guard, top_ref, mixed_ref, rows):
    parts = []
    highest = None
    for number in range(len(keys)):
        scores = lax.dot_general(
            queries, keys[number], (((1,), (1,)), ((), ())), preferred_element_type=jnp.float32
        )
        scores = scores * SCALE
        if allowed is not None:
            scores = jnp.where(allowed[number], scores, LOWEST)
        parts.append(scores)
        for begin in range(0, scores.shape[1], HD):
            piece = scores[:, begin : begin + HD]
            highest = piece if highest is None else jnp.maximum(highest, piece)
    before = top_ref[rows, :]
    top = jnp.maximum(before, jnp.max(highest, axis=1, keepdims=True))
    factor = jnp.exp2(before - top)
    mixed = mixed_ref[rows, :] * jnp.concatenate([factor, factor], axis=1)
    for number in range(len(keys)):
        width = parts[number].shape[1]
        lifted = jnp.concatenate([top] * (width // HD), axis=1)
        weight = jnp.exp2(parts[number] - lifted)
        if guard:
            weight = jnp.where(allowed[number], weight, 0.0)
        mixed = mixed + jnp.dot(
            weight.astype(jnp.bfloat16), values[number], preferred_element_type=jnp.float32
        )
    top_ref[rows, :] = top
    mixed_ref[rows, :] = mixed


def per_row(table, begin):
    seat = lax.broadcasted_iota(jnp.int32, (ROW, HD), 0)
    found = jnp.zeros((ROW, HD), jnp.int32)
    for row in range(ROW):
        found = jnp.where(seat == row, table[begin + row], found)
    return found


def head_rows(pack):
    rows = pack[TOK : TOK + ROW, :]
    return [rows[:, head * HD : (head + 1) * HD] for head in range(GROUP)]


def reach_of(pack):
    coded = pack[TOK + ROW :, : 2 * HD].astype(jnp.float32)
    return coded[:, :HD] * 64.0 + coded[:, HD:]


def diagonal():
    row = lax.broadcasted_iota(jnp.int32, (HD, HD), 0)
    return row == lax.broadcasted_iota(jnp.int32, (HD, HD), 1)


def seal(top_ref, mixed_ref, begin, count, to, packed, levels):
    rows = slice(begin, begin + count)
    mixed = mixed_ref[rows, :]
    amount = mixed[:, HD:]
    some = amount > 0.0
    safe = jnp.where(some, amount, 1.0)
    packed[to : to + count, :] = (mixed[:, :HD] / safe).astype(jnp.bfloat16)
    level = jnp.where(some, top_ref[rows, :] + jnp.log2(safe), LOWEST)
    seat = lax.broadcasted_iota(jnp.int32, levels.shape, 0)
    for start in range(0, count, HD):
        flat = jnp.sum(
            jnp.where(diagonal(), level[start : start + HD, :], 0.0), axis=0, keepdims=True
        )
        levels = jnp.where(seat == (to + start) // HD, flat, levels)
    return levels


def stage_kernel(plan, place_ref, *refs):
    refs = list(refs)
    init, finish, extra = plan["init"], plan["finish"], plan["extra"]
    own, mate, carrier = plan["own"], plan["mate"], plan["carrier"]
    rows_too = carrier is not None or extra
    node_ref = refs.pop(0) if extra else None
    blocks = [refs.pop(0) for _ in plan["counts"]]
    own_pack = refs.pop(0)
    mate_pack = refs.pop(0) if mate or rows_too else None
    if extra:
        rim, row_pairs = refs.pop(0), refs.pop(0)
    if not init:
        refs = refs[2 * (own + mate + rows_too) :]
    packed = refs.pop(0) if finish else None
    if own:
        own_top, own_mixed = refs.pop(0), refs.pop(0)
    if mate:
        mate_top, mate_mixed = refs.pop(0), refs.pop(0)
    if rows_too:
        rows_top, rows_mixed = refs.pop(0), refs.pop(0)
    keys, values, own_list, mate_list, loose_list, numbers = refs
    place = place_ref[0]
    mate_place = place + RUN - 2 * RUN * ((place // RUN) % 2)
    y, z = (place // RUN) % RING_Y, (place // (RING_Y * RUN)) * RUN + place % RUN

    slot = 0
    for block, count in zip(blocks, plan["counts"]):
        for number in range(count):
            held = slice(slot * TOK, (slot + 1) * TOK)
            here = slice(number * TOK, (number + 1) * TOK)
            keys[held, :] = block[here, :HD]
            values[held, :HD] = block[here, HD:]
            slot += 1
    values[:, HD:] = jnp.ones((values.shape[0], HD), jnp.bfloat16)

    if rows_too:
        decode_query = jnp.concatenate(head_rows(own_pack) + head_rows(mate_pack), axis=0)
    if carrier is not None:
        own_reach, mate_reach = reach_of(own_pack), reach_of(mate_pack)
        longest = jnp.max(jnp.maximum(own_reach, mate_reach))
        lane = lax.broadcasted_iota(jnp.int32, (ROW, TOK), 1).astype(jnp.float32)

    own_count, mate_count, loose_count = jnp.int32(0), jnp.int32(0), jnp.int32(0)
    for slot, (dz, other) in enumerate(plan["offsets"]):
        far_y, far_z = (RING_Y - 1 - y) if other else y, (z + dz + RING_Z) % RING_Z
        number = (far_z // RUN) * (RING_Y * RUN) + far_y * RUN + far_z % RUN
        numbers[slot] = number
        own_list[own_count] = jnp.int32(slot)
        own_count = own_count + (number < place).astype(jnp.int32)
        mate_list[mate_count] = jnp.int32(slot)
        mate_count = mate_count + (number < mate_place).astype(jnp.int32)
        if carrier is not None:
            bound = mate_place if carrier == "mate" else place
            left = (number >= bound) & ((number * TOK).astype(jnp.float32) < longest)
            loose_list[loose_count] = jnp.int32(slot)
            loose_count = loose_count + left.astype(jnp.int32)

    def load(slots):
        spans = [pl.ds(pl.multiple_of(slot * TOK, TOK), TOK) for slot in slots]
        return [keys[span, :] for span in spans], [values[span, :] for span in spans]

    def decode(slots, some_keys, some_values):
        allowed = []
        for slot in slots:
            base = (numbers[slot] * TOK).astype(jnp.float32)
            fits = []
            for reach in (own_reach, mate_reach):
                left = reach - base
                fits += [lane < jnp.concatenate([left, left], axis=1)] * GROUP
            allowed.append(jnp.concatenate(fits, axis=0))
        attend(
            decode_query,
            some_keys,
            some_values,
            allowed,
            True,
            rows_top,
            rows_mixed,
            slice(0, 2 * GROUP * ROW),
        )

    def prefill(pack, some_keys, some_values, allowed, top_ref, mixed_ref):
        for head in range(GROUP):
            attend(
                pack[:TOK, head * HD : (head + 1) * HD],
                some_keys,
                some_values,
                allowed,
                False,
                top_ref,
                mixed_ref,
                slice(head * TOK, (head + 1) * TOK),
            )

    fresh = [(own_top, own_mixed)] if init and own else []
    fresh += [(mate_top, mate_mixed), (rows_top, rows_mixed)] if init and mate else []
    for top_ref, mixed_ref in fresh:
        top_ref[...] = jnp.full(top_ref.shape, LOWEST, jnp.float32)
        mixed_ref[...] = jnp.zeros(mixed_ref.shape, jnp.float32)
    if init and own:
        token = lax.broadcasted_iota(jnp.int32, (TOK, TOK), 0)
        causal = [lax.broadcasted_iota(jnp.int32, (TOK, TOK), 1) <= token]
        some_keys, some_values = [keys[:TOK, :]], [values[:TOK, :]]
        prefill(own_pack, some_keys, some_values, causal, own_top, own_mixed)

    def sweep(pack, listed, count, top_ref, mixed_ref, with_rows):
        def turn_of(size):
            def turn(number, carry):
                slots = [listed[size * number + i] for i in range(size)]
                some_keys, some_values = load(slots)
                prefill(pack, some_keys, some_values, None, top_ref, mixed_ref)
                if with_rows:
                    decode(slots, some_keys, some_values)
                return carry

            return turn

        size = min(4, len(plan["offsets"]))
        if size > 1:
            lax.fori_loop(0, count // size, turn_of(size), 0)
        lax.fori_loop((count // size) * size, count, turn_of(1), 0)

    if own and not init:
        sweep(own_pack, own_list, own_count, own_top, own_mixed, carrier == "own")
    if mate:
        sweep(mate_pack, mate_list, mate_count, mate_top, mate_mixed, carrier == "mate")
    if carrier is not None:

        def rows_only(turn, carry):
            slots = [loose_list[turn]]
            decode(slots, *load(slots))
            return carry

        lax.fori_loop(0, loose_count, rows_only, 0)

    if extra:
        nodes = per_row(node_ref, place * ROW)
        seat = lax.broadcasted_iota(jnp.int32, (ROW, HD), 0)
        column = lax.broadcasted_iota(jnp.int32, (ROW, HD), 1)
        key_nodes = jnp.full((ROW, HD), -1, jnp.int32)
        previous = jnp.maximum(place - 1, 0) * ROW
        for row in range(ROW):
            rim_node = jnp.where(place > 0, node_ref[previous + row], -1)
            key_nodes = jnp.where(column == row, rim_node, key_nodes)
            key_nodes = jnp.where(column == ROW + row, node_ref[place * ROW + row], key_nodes)
        same = (key_nodes == nodes) & (column <= seat + ROW)
        pad = jnp.zeros((HD - 2 * ROW, HD), jnp.bfloat16)
        ones = jnp.ones((HD, HD), jnp.bfloat16)
        extra_keys = jnp.concatenate([rim[:, :HD], row_pairs[:, :HD], pad], axis=0)
        extra_values = jnp.concatenate([rim[:, HD:], row_pairs[:, HD:], pad], axis=0)
        attend(
            decode_query[: GROUP * ROW],
            [extra_keys],
            [jnp.concatenate([extra_values, ones], axis=1)],
            [jnp.concatenate([same] * GROUP, axis=0)],
            True,
            rows_top,
            rows_mixed,
            slice(0, GROUP * ROW),
        )

    if finish:
        levels = jnp.zeros((LEVELS, HD), jnp.float32)
        for head in range(GROUP):
            levels = seal(mate_top, mate_mixed, head * TOK, TOK, head * TOK, packed, levels)
        levels = seal(rows_top, rows_mixed, GROUP * ROW, HD, GROUP * TOK, packed, levels)
        for part in range(3):
            rounded = levels.astype(jnp.bfloat16)
            begin = HEIGHT + part * LEVELS
            packed[begin : begin + LEVELS, :] = rounded
            levels = levels - rounded.astype(jnp.float32)


def stage(
    place,
    packs,
    blocks,
    offsets,
    state,
    init=False,
    own=False,
    mate=False,
    carrier=None,
    finish=False,
    extra=None,
):
    rows_too = carrier is not None or extra is not None
    plan = dict(
        counts=[block.shape[0] // TOK for block in blocks],
        offsets=offsets,
        init=init,
        own=own,
        mate=mate,
        carrier=carrier,
        finish=finish,
        extra=extra is not None,
    )
    total = len(offsets)
    smem = [place] + ([extra[0]] if extra else [])
    packs = list(packs) if mate or rows_too else [packs[0]]
    operands = smem + list(blocks) + packs + (list(extra[1:]) if extra else [])
    used = [name for name, flag in (("own", own), ("mate", mate), ("rows", rows_too)) if flag]
    sizes = dict(own=GROUP * TOK, mate=GROUP * TOK, rows=2 * GROUP * ROW)
    shapes = [jax.ShapeDtypeStruct((HEIGHT + 3 * LEVELS, HD), jnp.bfloat16)] if finish else []
    aliases = {}
    for name in used:
        for index, width in enumerate((HD, 2 * HD)):
            if not init:
                aliases[len(operands)] = len(shapes)
                operands.append(state[name][index])
            shapes.append(jax.ShapeDtypeStruct((sizes[name], width), jnp.float32))
    work = total * TOK * TOK * GROUP * (own + mate)
    results = pl.pallas_call(
        functools.partial(stage_kernel, plan),
        in_specs=[IN_SMEM] * len(smem) + [IN_VMEM] * (len(operands) - len(smem)),
        out_specs=[IN_VMEM] * len(shapes),
        out_shape=shapes,
        scratch_shapes=[
            pltpu.VMEM((total * TOK, HD), jnp.bfloat16),
            pltpu.VMEM((total * TOK, 2 * HD), jnp.bfloat16),
        ]
        + [pltpu.SMEM((16,), jnp.int32) for _ in range(4)],
        input_output_aliases=aliases,
        compiler_params=pltpu.CompilerParams(vmem_limit_bytes=VMEM),
        cost_estimate=pl.CostEstimate(
            flops=work * 8 * HD, bytes_accessed=2000000, transcendentals=work
        ),
    )(*operands)
    results = list(results)
    packed = results.pop(0) if finish else None
    state = dict(state or {})
    for name in used:
        state[name] = (results.pop(0), results.pop(0))
    return (state, packed) if finish else state


def merge_kernel(own_top, own_mixed, rows_top, rows_mixed, packed, out, out_rows):
    levels = jnp.zeros((LEVELS, HD), jnp.float32)
    for part in range(3):
        begin = HEIGHT + part * LEVELS
        levels = levels + packed[begin : begin + LEVELS, :].astype(jnp.float32)

    def joined(top_ref, mixed_ref, begin, at):
        rows = slice(begin, begin + HD)
        flat = levels[at // HD : at // HD + 1, :]
        level = jnp.sum(jnp.where(diagonal(), flat, 0.0), axis=1, keepdims=True)
        top = top_ref[rows, :]
        highest = jnp.maximum(top, level)
        mine, theirs = jnp.exp2(top - highest), jnp.exp2(level - highest)
        mixed = mixed_ref[rows, :]
        other = packed[at : at + HD, :].astype(jnp.float32)
        amount = mine * mixed[:, HD:] + theirs
        return ((mine * mixed[:, :HD] + theirs * other) / amount).astype(jnp.bfloat16)

    for head in range(GROUP):
        for start in range(0, TOK, HD):
            begin = head * TOK + start
            part = joined(own_top, own_mixed, begin, begin)
            out[start : start + HD, head * HD : (head + 1) * HD] = part
    part = joined(rows_top, rows_mixed, 0, GROUP * TOK)
    for head in range(GROUP):
        out_rows[:, head * HD : (head + 1) * HD] = part[head * ROW : (head + 1) * ROW, :]


def merge(state, packed):
    return pl.pallas_call(
        merge_kernel,
        in_specs=[IN_VMEM] * 5,
        out_specs=[IN_VMEM] * 2,
        out_shape=[
            jax.ShapeDtypeStruct((TOK, GROUP * HD), jnp.bfloat16),
            jax.ShapeDtypeStruct((ROW, GROUP * HD), jnp.bfloat16),
        ],
        compiler_params=pltpu.CompilerParams(vmem_limit_bytes=VMEM),
    )(*state["own"], *state["rows"], packed)


def per_device(
    hidden_context,
    hidden_rows,
    norm_gain,
    key_value_weight,
    value_bias,
    query_context,
    query_rows,
    context_length,
    row_node,
):
    weights = key_value_weight.reshape(D, 2 * HD)
    gain = norm_gain.reshape(8, WIDE)
    bias = value_bias.reshape(1, HD)
    tp = lax.axis_index("tp").astype(jnp.int32).reshape(1)
    place = lax.axis_index(PLACE).astype(jnp.int32).reshape(1)

    def swap(block, bits):
        return lax.ppermute(block, PLACE, [(i, i ^ bits) for i in range(32)])

    own = jnp.concatenate([hidden_context, hidden_rows], axis=0)
    low, high, twin = move_x(own, 1), move_x(own, -1), swap_core(own)
    digits = jnp.stack([context_length // 64, context_length % 64], axis=1)
    coded = jnp.repeat(digits.astype(jnp.bfloat16), HD, axis=1)
    coded = jnp.pad(coded, ((0, 0), (0, WIDE - 2 * HD)))
    own_pack = jnp.concatenate([query_context, query_rows, coded], axis=0)
    add = functools.partial(project, tp, gain)
    state = add(
        [[(hidden_context, 0, TOK), (hidden_rows, 0, ROW)], [(twin, 0, BOTH)]],
        [(0, 0), (0, 1)],
        weights,
    )
    low, high, state, own_pack = lax.optimization_barrier((low, high, state, own_pack))
    mate_pack = swap(own_pack, RUN)
    far_low, far_high = move_x(low[:TOP], 1), move_x(high[TOP:], -1)
    low_twin, high_twin = swap_core(low), swap_core(high)
    state, rest = add(
        [[(piece, 0, BOTH)] for piece in (low, high, low_twin, high_twin)],
        [(-1, 0), (1, 0), (-1, 1), (1, 1)],
        weights,
        later=[(2, 0), (2, 1)],
        state=state,
    )
    far_low, far_high, state, rest = lax.optimization_barrier((far_low, far_high, state, rest))
    far_twin = swap_core(jnp.concatenate([far_low, far_high], axis=0))
    far = [(far_low, 0, TOP), (far_high, 0, BOTH - TOP)]
    state = add([far], [(2, 0)], rest, held=[0], state=state)
    pairs, row_pairs = add(
        [[(far_twin, 0, BOTH)]], [(2, 1)], rest, held=[1], state=state, bias=bias
    )

    opposite = 3 * RUN
    run = functools.partial(stage, place, (own_pack, mate_pack))
    above, below = move(pairs, 1, 0), move(pairs, -1, 0)
    state = run([pairs], [(0, 0)], None, init=True, own=True)
    rim = lax.ppermute(row_pairs, PLACE, [(i, i + 1) for i in range(31)])
    above, below, state, rim = lax.optimization_barrier((above, below, state, rim))
    above_two, below_two = move(above, 1, 0), move(below, -1, 0)
    first = swap(jnp.concatenate([pairs, above, below], axis=0), opposite)
    state = run([above, below], [(-1, 0), (1, 0)], state, own=True)
    above_two, below_two, state, mate_pack = lax.optimization_barrier(
        (above_two, below_two, state, mate_pack)
    )
    run = functools.partial(stage, place, (own_pack, mate_pack))
    above_three, below_three = move(above_two, 1, 0), move(below_two, -1, 0)
    second = swap(jnp.concatenate([above_two, below_two], axis=0), opposite)
    line = [pairs, above, below, above_two, below_two]
    steps = [(0, 0), (-1, 0), (1, 0), (-2, 0), (2, 0)]
    state = run(line, steps, state, init=True, mate=True, carrier="mate")
    above_three, below_three, state = lax.optimization_barrier((above_three, below_three, state))
    ends = [move(above_three[:TOP], 1, 0), move(below_three[TOP:], -1, 0)]
    third = swap(jnp.concatenate([above_three, below_three], axis=0), opposite)
    across = [first, second]
    across_steps = [(0, 1), (-1, 1), (1, 1), (-2, 1), (2, 1)]
    state = run(across, across_steps, state, mate=True, carrier="mate")
    ends, state = lax.optimization_barrier((ends, state))
    end = jnp.concatenate(ends, axis=0)
    fourth = swap(end, opposite)
    late, late_steps = [above_three, below_three, end], [(-3, 0), (3, 0), (4, 0)]
    state = run(late, late_steps, state, mate=True, carrier="mate")
    last, last_steps = [third, fourth], [(-3, 1), (3, 1), (4, 1)]
    state, packed = run(last, last_steps, state, mate=True, carrier="mate", finish=True)
    sent = swap(packed, RUN)
    packed, state = lax.optimization_barrier((packed, state))
    state = run(
        line[3:] + across + late + last,
        steps[3:] + across_steps + late_steps + last_steps,
        state,
        own=True,
        extra=(row_node, rim, row_pairs),
    )
    out, out_rows = merge(state, sent)
    return out, out_rows


def solution(mesh):
    return jax.shard_map(
        per_device,
        mesh=mesh,
        in_specs=(
            P(PLACE, "tp"),
            P(PLACE, "tp"),
            P(),
            P(None, None, "tp"),
            P("tp"),
            P(PLACE, "tp"),
            P(PLACE, "tp"),
            P(PLACE),
            P(),
        ),
        out_specs=(P(PLACE, "tp"), P(PLACE, "tp")),
        check_vma=False,
    )
```

```python
import functools
import math

import jax
import jax.numpy as jnp
from jax import lax
from jax.experimental import pallas as pl
from jax.experimental.pallas import tpu as pltpu
from jax.sharding import PartitionSpec as P

D = 8192
H = 64
KVH = 8
HD = 128
STEPS = 4
GROUP = H // KVH

PLACE = ("sec", "seq")
RING_Z, RING_Y, RUN = 8, 4, 4
TOK = 256
ROW = 16
BOTH = TOK + ROW
TOP = 128
WIDE = 1024
HEIGHT = GROUP * (TOK + ROW)
LEVELS = 32
LOWEST = -1e30
SCALE = math.log2(math.e) / math.sqrt(HD)
VMEM = 32 * 1024 * 1024
IN_VMEM = pl.BlockSpec(memory_space=pltpu.VMEM)
IN_SMEM = pl.BlockSpec(memory_space=pltpu.SMEM)
IN_HBM = pl.BlockSpec(memory_space=pltpu.HBM)


def place_of(y, z):
    return (z // RUN) * (RING_Y * RUN) + y * RUN + z % RUN


def move(block, dz, dy):
    route = [
        (place_of(y, z), place_of((y + dy) % RING_Y, (z + dz) % RING_Z))
        for y in range(RING_Y)
        for z in range(RING_Z)
    ]
    return lax.ppermute(block, PLACE, route)


def move_x(block, step):
    return lax.ppermute(block, "tp", [(i, (i + 2 * step) % 8) for i in range(8)])


def swap_core(block):
    return lax.ppermute(block, "tp", [(i, i ^ 1) for i in range(8)])


def project_kernel(spans, shifts, later, held, first, last, tp_ref, *refs):
    refs = list(refs)
    pieces = [[(refs.pop(0), *span) for span in piece] for piece in spans]
    weights, gain = refs.pop(0), refs.pop(0)
    if not first:
        product_in, squares_in = refs.pop(0), refs.pop(0)
    if last:
        bias = refs.pop(0)
    tp = tp_ref[0]
    mate = tp + 1 - 2 * (tp % 2)

    def owner_of(shift):
        step, other = shift
        return ((mate if other else tp) + 2 * step + 8) % 8

    copies = []
    if held is None:
        ready, slices = refs.pop(), refs.pop()
        for number, shift in enumerate(shifts + later):
            rows = pl.ds(pl.multiple_of(owner_of(shift) * WIDE, WIDE), WIDE)
            far = number - len(shifts)
            to = slices.at[number] if far < 0 else refs[2].at[far]
            copies.append(pltpu.make_async_copy(weights.at[rows, :], to, ready.at[number]))
            copies[-1].start()
    else:
        slices = weights
    product = jnp.zeros((BOTH, 2 * HD), jnp.float32) if first else product_in[...]
    squares = jnp.zeros((BOTH, HD), jnp.float32) if first else squares_in[...]
    for number, (piece, shift) in enumerate(zip(pieces, shifts)):
        if held is None:
            copies[number].wait()
        slot = number if held is None else held[number]

        def chunk(turn, carry, piece=piece, slot=slot, owner=owner_of(shift)):
            product, squares = carry
            span = pl.ds(pl.multiple_of(turn * 256, 256), 256)
            chunks = [ref[pl.ds(start, stop - start), span] for ref, start, stop in piece]
            wide = jnp.concatenate(chunks, axis=0).astype(jnp.float32)
            squared = wide * wide
            squares = squares + (squared[:, :HD] + squared[:, HD:])
            scaled = (wide * gain[pl.ds(owner, 1), span]).astype(jnp.bfloat16)
            return (
                product
                + jnp.dot(scaled, slices[slot, span, :], preferred_element_type=jnp.float32),
                squares,
            )

        if len(pieces) == 1:
            for number in range(WIDE // 256):
                product, squares = chunk(number, (product, squares))
        else:
            product, squares = lax.fori_loop(0, WIDE // 256, chunk, (product, squares))
    for copy in copies[len(shifts) :]:
        copy.wait()
    if not last:
        refs[0][...] = product
        refs[1][...] = squares
        return
    inverse = lax.rsqrt(jnp.sum(squares, axis=1, keepdims=True) / D + 1e-06)
    keys = (product[:, :HD] * inverse).astype(jnp.bfloat16)
    values = (product[:, HD:] * inverse + bias[...]).astype(jnp.bfloat16)
    refs[0][:, :HD] = keys[:TOK]
    refs[0][:, HD:] = values[:TOK]
    refs[1][:, :HD] = keys[TOK:]
    refs[1][:, HD:] = values[TOK:]


def project(tp, gain, pieces, shifts, weights, later=(), held=None, state=None, bias=None):
    spans = [[(start, stop) for _, start, stop in piece] for piece in pieces]
    count, later = len(pieces), list(later)
    first, last = state is None, bias is not None
    operands = [tp] + [chunk[0] for piece in pieces for chunk in piece] + [weights, gain]
    specs = [IN_SMEM] + [IN_VMEM] * (len(operands) - 3)
    specs += [IN_HBM if held is None else IN_VMEM, IN_VMEM]
    if not first:
        operands += list(state)
    if last:
        operands.append(bias)
        shapes = [
            jax.ShapeDtypeStruct((TOK, 2 * HD), jnp.bfloat16),
            jax.ShapeDtypeStruct((ROW, 2 * HD), jnp.bfloat16),
        ]
    else:
        shapes = [
            jax.ShapeDtypeStruct((BOTH, 2 * HD), jnp.float32),
            jax.ShapeDtypeStruct((BOTH, HD), jnp.float32),
        ]
    if later:
        shapes.append(jax.ShapeDtypeStruct((len(later), WIDE, 2 * HD), jnp.bfloat16))
    scratch = []
    if held is None:
        scratch = [
            pltpu.VMEM((count, WIDE, 2 * HD), jnp.bfloat16),
            pltpu.SemaphoreType.DMA((count + len(later),)),
        ]
    specs += [IN_VMEM] * (len(operands) - len(specs))
    results = pl.pallas_call(
        functools.partial(project_kernel, spans, shifts, later, held, first, last),
        in_specs=specs,
        out_specs=[IN_VMEM] * len(shapes),
        out_shape=shapes,
        scratch_shapes=scratch,
        compiler_params=pltpu.CompilerParams(vmem_limit_bytes=VMEM),
        cost_estimate=pl.CostEstimate(
            flops=count * BOTH * WIDE * 512,
            bytes_accessed=count * 1100000,
            transcendentals=0,
        ),
    )(*operands)
    return (tuple(results[:2]), results[2]) if later else tuple(results)


def attend(queries, keys, values, allowed, guard, top_ref, mixed_ref, rows, active=None):
    parts = []
    highest = None
    for number in range(len(keys)):
        scores = lax.dot_general(
            queries, keys[number], (((1,), (1,)), ((), ())), preferred_element_type=jnp.float32
        )
        scores = scores * SCALE
        if allowed is not None:
            scores = jnp.where(allowed[number], scores, LOWEST)
        parts.append(scores)
        for begin in range(0, scores.shape[1], HD):
            piece = scores[:, begin : begin + HD]
            highest = piece if highest is None else jnp.maximum(highest, piece)
    before = top_ref[rows, :]
    top = jnp.maximum(before, jnp.max(highest, axis=1, keepdims=True))
    factor = jnp.exp2(before - top)
    earlier = mixed_ref[rows, :]
    mixed = earlier * jnp.concatenate([factor, factor], axis=1)
    for number in range(len(keys)):
        width = parts[number].shape[1]
        lifted = jnp.concatenate([top] * (width // HD), axis=1)
        weight = jnp.exp2(parts[number] - lifted)
        if guard:
            weight = jnp.where(allowed[number], weight, 0.0)
        mixed = mixed + jnp.dot(
            weight.astype(jnp.bfloat16), values[number], preferred_element_type=jnp.float32
        )
    if active is not None:
        top, mixed = jnp.where(active, top, before), jnp.where(active, mixed, earlier)
    top_ref[rows, :] = top
    mixed_ref[rows, :] = mixed


def per_row(table, begin):
    seat = lax.broadcasted_iota(jnp.int32, (ROW, HD), 0)
    found = jnp.zeros((ROW, HD), jnp.int32)
    for row in range(ROW):
        found = jnp.where(seat == row, table[begin + row], found)
    return found


def head_rows(pack):
    rows = pack[TOK : TOK + ROW, :]
    return [rows[:, head * HD : (head + 1) * HD] for head in range(GROUP)]


def reach_of(pack):
    coded = pack[TOK + ROW :, : 2 * HD].astype(jnp.float32)
    return coded[:, :HD] * 64.0 + coded[:, HD:]


def diagonal():
    row = lax.broadcasted_iota(jnp.int32, (HD, HD), 0)
    return row == lax.broadcasted_iota(jnp.int32, (HD, HD), 1)


def seal(top_ref, mixed_ref, begin, count, to, packed, levels):
    rows = slice(begin, begin + count)
    mixed = mixed_ref[rows, :]
    amount = mixed[:, HD:]
    some = amount > 0.0
    safe = jnp.where(some, amount, 1.0)
    packed[to : to + count, :] = (mixed[:, :HD] / safe).astype(jnp.bfloat16)
    level = jnp.where(some, top_ref[rows, :] + jnp.log2(safe), LOWEST)
    seat = lax.broadcasted_iota(jnp.int32, levels.shape, 0)
    for start in range(0, count, HD):
        flat = jnp.sum(
            jnp.where(diagonal(), level[start : start + HD, :], 0.0), axis=0, keepdims=True
        )
        levels = jnp.where(seat == (to + start) // HD, flat, levels)
    return levels


def stage_kernel(plan, place_ref, *refs):
    refs = list(refs)
    init, finish, extra = plan["init"], plan["finish"], plan["extra"]
    own, mate, carrier = plan["own"], plan["mate"], plan["carrier"]
    rows_too = carrier is not None or extra
    node_ref = refs.pop(0) if extra else None
    blocks = [refs.pop(0) for _ in plan["counts"]]
    own_pack = refs.pop(0)
    mate_pack = refs.pop(0) if mate or rows_too else None
    if extra:
        rim, row_pairs = refs.pop(0), refs.pop(0)
    if not init:
        refs = refs[2 * (own + mate + rows_too) :]
    packed = refs.pop(0) if finish else None
    if own:
        own_top, own_mixed = refs.pop(0), refs.pop(0)
    if mate:
        mate_top, mate_mixed = refs.pop(0), refs.pop(0)
    if rows_too:
        rows_top, rows_mixed = refs.pop(0), refs.pop(0)
    keys, values, raw_keys, raw_values, numbers = refs
    place = place_ref[0]
    mate_place = place + RUN - 2 * RUN * ((place // RUN) % 2)
    y, z = (place // RUN) % RING_Y, (place // (RING_Y * RUN)) * RUN + place % RUN
    size = plan["size"]
    bound = mate_place if mate else place
    ones = jnp.ones((TOK, HD), jnp.bfloat16)

    def span_of(slot):
        return pl.ds(pl.multiple_of(slot * TOK, TOK), TOK)

    slot, count = 0, jnp.int32(0)
    for block, amount in zip(blocks, plan["counts"]):
        for part in range(amount):
            dz, other = plan["offsets"][slot]
            far_y, far_z = (RING_Y - 1 - y) if other else y, (z + dz + RING_Z) % RING_Z
            number = (far_z // RUN) * (RING_Y * RUN) + far_y * RUN + far_z % RUN
            numbers[slot] = number
            key = block[part * TOK : (part + 1) * TOK, :HD]
            value = jnp.concatenate([block[part * TOK : (part + 1) * TOK, HD:], ones], axis=1)
            if carrier is not None:
                raw_keys[slot * TOK : (slot + 1) * TOK, :] = key
                raw_values[slot * TOK : (slot + 1) * TOK, :] = value
            keys[span_of(count), :] = key
            values[span_of(count), :] = value
            count = count + (number < bound).astype(jnp.int32)
            slot += 1
    if not (init and own):
        for more in range(size - 1):
            keys[span_of(count + more), :] = keys[:TOK, :]
            values[span_of(count + more), :] = jnp.zeros((TOK, 2 * HD), jnp.bfloat16)

    if rows_too:
        decode_query = jnp.concatenate(head_rows(own_pack) + head_rows(mate_pack), axis=0)
    if carrier is not None:
        own_reach, mate_reach = reach_of(own_pack), reach_of(mate_pack)
        lane = lax.broadcasted_iota(jnp.int32, (ROW, TOK), 1).astype(jnp.float32)

    def decode():
        allowed = []
        for slot in range(len(plan["offsets"])):
            base = (numbers[slot] * TOK).astype(jnp.float32)
            fits = []
            for reach in (own_reach, mate_reach):
                left = reach - base
                fits += [lane < jnp.concatenate([left, left], axis=1)] * GROUP
            allowed.append(jnp.concatenate(fits, axis=0))
        spans = [slice(i * TOK, (i + 1) * TOK) for i in range(len(plan["offsets"]))]
        attend(
            decode_query,
            [raw_keys[span, :] for span in spans],
            [raw_values[span, :] for span in spans],
            allowed,
            True,
            rows_top,
            rows_mixed,
            slice(0, 2 * GROUP * ROW),
        )

    def prefill(pack, some_keys, some_values, allowed, top_ref, mixed_ref, at_once, active=None):
        def some_heads(turn, carry):
            for number in range(at_once):
                head = turn * at_once + number
                lanes = pl.ds(pl.multiple_of(head * HD, HD), HD)
                attend(
                    pack[pl.ds(0, TOK), lanes],
                    some_keys,
                    some_values,
                    allowed,
                    False,
                    top_ref,
                    mixed_ref,
                    pl.ds(pl.multiple_of(head * TOK, TOK), TOK),
                    active,
                )
            return carry

        if at_once == GROUP:
            some_heads(0, 0)
        else:
            lax.fori_loop(0, GROUP // at_once, some_heads, 0)

    fresh = [(own_top, own_mixed)] if init and own else []
    fresh += [(mate_top, mate_mixed), (rows_top, rows_mixed)] if init and mate else []
    for top_ref, mixed_ref in fresh:
        top_ref[...] = jnp.full(top_ref.shape, LOWEST, jnp.float32)
        mixed_ref[...] = jnp.zeros(mixed_ref.shape, jnp.float32)
    if init and own:
        token = lax.broadcasted_iota(jnp.int32, (TOK, TOK), 0)
        causal = [lax.broadcasted_iota(jnp.int32, (TOK, TOK), 1) <= token]
        prefill(own_pack, [keys[:TOK, :]], [values[:TOK, :]], causal, own_top, own_mixed, 4)
    else:
        pack = mate_pack if mate else own_pack
        top_ref, mixed_ref = (mate_top, mate_mixed) if mate else (own_top, own_mixed)

        def turn(number, carry, active=None):
            spans = [span_of(number * size + i) for i in range(size)]
            some_keys = [keys[span, :] for span in spans]
            some_values = [values[span, :] for span in spans]
            at_once = plan["at_once"]
            prefill(pack, some_keys, some_values, None, top_ref, mixed_ref, at_once, active)
            return carry

        if carrier is None:
            lax.fori_loop(0, (count + size - 1) // size, turn, 0)
        else:
            turn(0, 0, count > 0)
            decode()

    if extra:
        nodes = per_row(node_ref, place * ROW)
        seat = lax.broadcasted_iota(jnp.int32, (ROW, HD), 0)
        column = lax.broadcasted_iota(jnp.int32, (ROW, HD), 1)
        key_nodes = jnp.full((ROW, HD), -1, jnp.int32)
        previous = jnp.maximum(place - 1, 0) * ROW
        for row in range(ROW):
            rim_node = jnp.where(place > 0, node_ref[previous + row], -1)
            key_nodes = jnp.where(column == row, rim_node, key_nodes)
            key_nodes = jnp.where(column == ROW + row, node_ref[place * ROW + row], key_nodes)
        same = (key_nodes == nodes) & (column <= seat + ROW)
        pad = jnp.zeros((HD - 2 * ROW, HD), jnp.bfloat16)
        extra_ones = jnp.ones((HD, HD), jnp.bfloat16)
        extra_keys = jnp.concatenate([rim[:, :HD], row_pairs[:, :HD], pad], axis=0)
        extra_values = jnp.concatenate([rim[:, HD:], row_pairs[:, HD:], pad], axis=0)
        attend(
            decode_query[: GROUP * ROW],
            [extra_keys],
            [jnp.concatenate([extra_values, extra_ones], axis=1)],
            [jnp.concatenate([same] * GROUP, axis=0)],
            True,
            rows_top,
            rows_mixed,
            slice(0, GROUP * ROW),
        )

    if finish:
        levels = jnp.zeros((LEVELS, HD), jnp.float32)
        for head in range(GROUP):
            levels = seal(mate_top, mate_mixed, head * TOK, TOK, head * TOK, packed, levels)
        levels = seal(rows_top, rows_mixed, GROUP * ROW, HD, GROUP * TOK, packed, levels)
        for part in range(3):
            rounded = levels.astype(jnp.bfloat16)
            begin = HEIGHT + part * LEVELS
            packed[begin : begin + LEVELS, :] = rounded
            levels = levels - rounded.astype(jnp.float32)


def stage(
    place,
    packs,
    blocks,
    offsets,
    state,
    init=False,
    own=False,
    mate=False,
    carrier=None,
    finish=False,
    extra=None,
    at_once=4,
    size=5,
):
    rows_too = carrier is not None or extra is not None
    plan = dict(
        counts=[block.shape[0] // TOK for block in blocks],
        offsets=offsets,
        init=init,
        own=own,
        mate=mate,
        carrier=carrier,
        finish=finish,
        extra=extra is not None,
        at_once=at_once,
        size=size,
    )
    total = len(offsets)
    smem = [place] + ([extra[0]] if extra else [])
    packs = list(packs) if mate or rows_too else [packs[0]]
    operands = smem + list(blocks) + packs + (list(extra[1:]) if extra else [])
    used = [name for name, flag in (("own", own), ("mate", mate), ("rows", rows_too)) if flag]
    sizes = dict(own=GROUP * TOK, mate=GROUP * TOK, rows=2 * GROUP * ROW)
    shapes = [jax.ShapeDtypeStruct((HEIGHT + 3 * LEVELS, HD), jnp.bfloat16)] if finish else []
    aliases = {}
    for name in used:
        for index, width in enumerate((HD, 2 * HD)):
            if not init:
                aliases[len(operands)] = len(shapes)
                operands.append(state[name][index])
            shapes.append(jax.ShapeDtypeStruct((sizes[name], width), jnp.float32))
    work = total * TOK * TOK * GROUP * (own + mate)
    results = pl.pallas_call(
        functools.partial(stage_kernel, plan),
        in_specs=[IN_SMEM] * len(smem) + [IN_VMEM] * (len(operands) - len(smem)),
        out_specs=[IN_VMEM] * len(shapes),
        out_shape=shapes,
        scratch_shapes=[
            pltpu.VMEM(((total + size) * TOK, HD), jnp.bfloat16),
            pltpu.VMEM(((total + size) * TOK, 2 * HD), jnp.bfloat16),
            pltpu.VMEM((total * TOK, HD), jnp.bfloat16),
            pltpu.VMEM((total * TOK, 2 * HD), jnp.bfloat16),
            pltpu.SMEM((16,), jnp.int32),
        ],
        input_output_aliases=aliases,
        compiler_params=pltpu.CompilerParams(vmem_limit_bytes=VMEM),
        cost_estimate=pl.CostEstimate(
            flops=work * 8 * HD, bytes_accessed=2000000, transcendentals=work
        ),
    )(*operands)
    results = list(results)
    packed = results.pop(0) if finish else None
    state = dict(state or {})
    for name in used:
        state[name] = (results.pop(0), results.pop(0))
    return (state, packed) if finish else state


def merge_kernel(own_top, own_mixed, rows_top, rows_mixed, packed, out, out_rows):
    levels = jnp.zeros((LEVELS, HD), jnp.float32)
    for part in range(3):
        begin = HEIGHT + part * LEVELS
        levels = levels + packed[begin : begin + LEVELS, :].astype(jnp.float32)

    def joined(top_ref, mixed_ref, begin, at):
        rows = slice(begin, begin + HD)
        flat = levels[at // HD : at // HD + 1, :]
        level = jnp.sum(jnp.where(diagonal(), flat, 0.0), axis=1, keepdims=True)
        top = top_ref[rows, :]
        highest = jnp.maximum(top, level)
        mine, theirs = jnp.exp2(top - highest), jnp.exp2(level - highest)
        mixed = mixed_ref[rows, :]
        other = packed[at : at + HD, :].astype(jnp.float32)
        amount = mine * mixed[:, HD:] + theirs
        return ((mine * mixed[:, :HD] + theirs * other) / amount).astype(jnp.bfloat16)

    for head in range(GROUP):
        for start in range(0, TOK, HD):
            begin = head * TOK + start
            part = joined(own_top, own_mixed, begin, begin)
            out[start : start + HD, head * HD : (head + 1) * HD] = part
    part = joined(rows_top, rows_mixed, 0, GROUP * TOK)
    for head in range(GROUP):
        out_rows[:, head * HD : (head + 1) * HD] = part[head * ROW : (head + 1) * ROW, :]


def merge(state, packed):
    return pl.pallas_call(
        merge_kernel,
        in_specs=[IN_VMEM] * 5,
        out_specs=[IN_VMEM] * 2,
        out_shape=[
            jax.ShapeDtypeStruct((TOK, GROUP * HD), jnp.bfloat16),
            jax.ShapeDtypeStruct((ROW, GROUP * HD), jnp.bfloat16),
        ],
        compiler_params=pltpu.CompilerParams(vmem_limit_bytes=VMEM),
    )(*state["own"], *state["rows"], packed)


def per_device(
    hidden_context,
    hidden_rows,
    norm_gain,
    key_value_weight,
    value_bias,
    query_context,
    query_rows,
    context_length,
    row_node,
):
    weights = key_value_weight.reshape(D, 2 * HD)
    gain = norm_gain.reshape(8, WIDE)
    bias = value_bias.reshape(1, HD)
    tp = lax.axis_index("tp").astype(jnp.int32).reshape(1)
    place = lax.axis_index(PLACE).astype(jnp.int32).reshape(1)

    def swap(block, bits):
        return lax.ppermute(block, PLACE, [(i, i ^ bits) for i in range(32)])

    own = jnp.concatenate([hidden_context, hidden_rows], axis=0)
    low, high, twin = move_x(own, 1), move_x(own, -1), swap_core(own)
    digits = jnp.stack([context_length // 64, context_length % 64], axis=1)
    coded = jnp.repeat(digits.astype(jnp.bfloat16), HD, axis=1)
    coded = jnp.pad(coded, ((0, 0), (0, WIDE - 2 * HD)))
    own_pack = jnp.concatenate([query_context, query_rows, coded], axis=0)
    add = functools.partial(project, tp, gain)
    state = add(
        [[(hidden_context, 0, TOK), (hidden_rows, 0, ROW)], [(twin, 0, BOTH)]],
        [(0, 0), (0, 1)],
        weights,
    )
    low, high, state, own_pack = lax.optimization_barrier((low, high, state, own_pack))
    mate_pack = swap(own_pack, RUN)
    far_low, far_high = move_x(low[:TOP], 1), move_x(high[TOP:], -1)
    low_twin, high_twin = swap_core(low), swap_core(high)
    state, rest = add(
        [[(piece, 0, BOTH)] for piece in (low, high, low_twin, high_twin)],
        [(-1, 0), (1, 0), (-1, 1), (1, 1)],
        weights,
        later=[(2, 0), (2, 1)],
        state=state,
    )
    far_low, far_high, state, rest = lax.optimization_barrier((far_low, far_high, state, rest))
    far_twin = swap_core(jnp.concatenate([far_low, far_high], axis=0))
    far = [(far_low, 0, TOP), (far_high, 0, BOTH - TOP)]
    state = add([far], [(2, 0)], rest, held=[0], state=state)
    pairs, row_pairs = add(
        [[(far_twin, 0, BOTH)]], [(2, 1)], rest, held=[1], state=state, bias=bias
    )

    opposite = 3 * RUN
    run = functools.partial(stage, place, (own_pack, mate_pack))
    above, below = move(pairs, 1, 0), move(pairs, -1, 0)
    state = run([pairs], [(0, 0)], None, init=True, own=True)
    rim = lax.ppermute(row_pairs, PLACE, [(i, i + 1) for i in range(31)])
    above, below, state, rim = lax.optimization_barrier((above, below, state, rim))
    above_two, below_two = move(above, 1, 0), move(below, -1, 0)
    first = swap(jnp.concatenate([pairs, above, below], axis=0), opposite)
    above_two, below_two, mate_pack = lax.optimization_barrier((above_two, below_two, mate_pack))
    run = functools.partial(stage, place, (own_pack, mate_pack))
    above_three, below_three = move(above_two, 1, 0), move(below_two, -1, 0)
    second = swap(jnp.concatenate([above_two, below_two], axis=0), opposite)
    line = [pairs, above, below, above_two, below_two]
    steps = [(0, 0), (-1, 0), (1, 0), (-2, 0), (2, 0)]
    state = run(line, steps, state, init=True, mate=True, carrier="mate")
    above_three, below_three, state = lax.optimization_barrier((above_three, below_three, state))
    ends = [move(above_three[:TOP], 1, 0), move(below_three[TOP:], -1, 0)]
    third = swap(jnp.concatenate([above_three, below_three], axis=0), opposite)
    across = [first, second]
    across_steps = [(0, 1), (-1, 1), (1, 1), (-2, 1), (2, 1)]
    state = run(across, across_steps, state, mate=True, carrier="mate", at_once=GROUP)
    ends, state = lax.optimization_barrier((ends, state))
    end = jnp.concatenate(ends, axis=0)
    fourth = swap(end, opposite)
    late, late_steps = [above_three, below_three, end], [(-3, 0), (3, 0), (4, 0)]
    state = run(late, late_steps, state, mate=True, carrier="mate", size=3)
    last, last_steps = [third, fourth], [(-3, 1), (3, 1), (4, 1)]
    state, packed = run(last, last_steps, state, mate=True, carrier="mate", finish=True, size=3)
    sent = swap(packed, RUN)
    packed, state = lax.optimization_barrier((packed, state))
    state = run(
        line[1:] + across + late + last,
        steps[1:] + across_steps + late_steps + last_steps,
        state,
        own=True,
        extra=(row_node, rim, row_pairs),
        at_once=GROUP,
    )
    out, out_rows = merge(state, sent)
    return out, out_rows


def solution(mesh):
    return jax.shard_map(
        per_device,
        mesh=mesh,
        in_specs=(
            P(PLACE, "tp"),
            P(PLACE, "tp"),
            P(),
            P(None, None, "tp"),
            P("tp"),
            P(PLACE, "tp"),
            P(PLACE, "tp"),
            P(PLACE),
            P(),
        ),
        out_specs=(P(PLACE, "tp"), P(PLACE, "tp")),
        check_vma=False,
    )
```

```python
import functools
import math

import jax
import jax.numpy as jnp
from jax import lax
from jax.experimental import pallas as pl
from jax.experimental.pallas import tpu as pltpu
from jax.sharding import PartitionSpec as P

D = 8192
H = 64
KVH = 8
HD = 128
STEPS = 4
GROUP = H // KVH

PLACE = ("sec", "seq")
RING_Z, RING_Y, RUN = 8, 4, 4
TOK = 256
ROW = 16
BOTH = TOK + ROW
TOP = 128
WIDE = 1024
HEIGHT = GROUP * (TOK + ROW)
LEVELS = 32
LOWEST = -1e30
SCALE = math.log2(math.e) / math.sqrt(HD)
VMEM = 32 * 1024 * 1024
IN_VMEM = pl.BlockSpec(memory_space=pltpu.VMEM)
IN_SMEM = pl.BlockSpec(memory_space=pltpu.SMEM)
IN_HBM = pl.BlockSpec(memory_space=pltpu.HBM)


def place_of(y, z):
    return (z // RUN) * (RING_Y * RUN) + y * RUN + z % RUN


def move(block, dz, dy):
    route = [
        (place_of(y, z), place_of((y + dy) % RING_Y, (z + dz) % RING_Z))
        for y in range(RING_Y)
        for z in range(RING_Z)
    ]
    return lax.ppermute(block, PLACE, route)


def move_x(block, step):
    return lax.ppermute(block, "tp", [(i, (i + 2 * step) % 8) for i in range(8)])


def swap_core(block):
    return lax.ppermute(block, "tp", [(i, i ^ 1) for i in range(8)])


def project_kernel(spans, shifts, later, held, first, last, tp_ref, *refs):
    refs = list(refs)
    pieces = [[(refs.pop(0), *span) for span in piece] for piece in spans]
    weights, gain = refs.pop(0), refs.pop(0)
    if not first:
        product_in, squares_in = refs.pop(0), refs.pop(0)
    if last:
        bias = refs.pop(0)
    tp = tp_ref[0]
    mate = tp + 1 - 2 * (tp % 2)

    def owner_of(shift):
        step, other = shift
        return ((mate if other else tp) + 2 * step + 8) % 8

    copies = []
    if held is None:
        ready, slices = refs.pop(), refs.pop()
        for number, shift in enumerate(shifts + later):
            rows = pl.ds(pl.multiple_of(owner_of(shift) * WIDE, WIDE), WIDE)
            far = number - len(shifts)
            to = slices.at[number] if far < 0 else refs[2].at[far]
            copies.append(pltpu.make_async_copy(weights.at[rows, :], to, ready.at[number]))
            copies[-1].start()
    else:
        slices = weights
    product = jnp.zeros((BOTH, 2 * HD), jnp.float32) if first else product_in[...]
    squares = jnp.zeros((BOTH, HD), jnp.float32) if first else squares_in[...]
    for number, (piece, shift) in enumerate(zip(pieces, shifts)):
        if held is None:
            copies[number].wait()
        slot = number if held is None else held[number]

        def chunk(turn, carry, piece=piece, slot=slot, owner=owner_of(shift)):
            product, squares = carry
            span = pl.ds(pl.multiple_of(turn * 256, 256), 256)
            chunks = [ref[pl.ds(start, stop - start), span] for ref, start, stop in piece]
            wide = jnp.concatenate(chunks, axis=0).astype(jnp.float32)
            squared = wide * wide
            squares = squares + (squared[:, :HD] + squared[:, HD:])
            scaled = (wide * gain[pl.ds(owner, 1), span]).astype(jnp.bfloat16)
            return (
                product
                + jnp.dot(scaled, slices[slot, span, :], preferred_element_type=jnp.float32),
                squares,
            )

        if len(pieces) == 1:
            for number in range(WIDE // 256):
                product, squares = chunk(number, (product, squares))
        else:
            product, squares = lax.fori_loop(0, WIDE // 256, chunk, (product, squares))
    for copy in copies[len(shifts) :]:
        copy.wait()
    if not last:
        refs[0][...] = product
        refs[1][...] = squares
        return
    inverse = lax.rsqrt(jnp.sum(squares, axis=1, keepdims=True) / D + 1e-06)
    keys = (product[:, :HD] * inverse).astype(jnp.bfloat16)
    values = (product[:, HD:] * inverse + bias[...]).astype(jnp.bfloat16)
    refs[0][:, :HD] = keys[:TOK]
    refs[0][:, HD:] = values[:TOK]
    refs[1][:, :HD] = keys[TOK:]
    refs[1][:, HD:] = values[TOK:]


def project(tp, gain, pieces, shifts, weights, later=(), held=None, state=None, bias=None):
    spans = [[(start, stop) for _, start, stop in piece] for piece in pieces]
    count, later = len(pieces), list(later)
    first, last = state is None, bias is not None
    operands = [tp] + [chunk[0] for piece in pieces for chunk in piece] + [weights, gain]
    specs = [IN_SMEM] + [IN_VMEM] * (len(operands) - 3)
    specs += [IN_HBM if held is None else IN_VMEM, IN_VMEM]
    if not first:
        operands += list(state)
    if last:
        operands.append(bias)
        shapes = [
            jax.ShapeDtypeStruct((TOK, 2 * HD), jnp.bfloat16),
            jax.ShapeDtypeStruct((ROW, 2 * HD), jnp.bfloat16),
        ]
    else:
        shapes = [
            jax.ShapeDtypeStruct((BOTH, 2 * HD), jnp.float32),
            jax.ShapeDtypeStruct((BOTH, HD), jnp.float32),
        ]
    if later:
        shapes.append(jax.ShapeDtypeStruct((len(later), WIDE, 2 * HD), jnp.bfloat16))
    scratch = []
    if held is None:
        scratch = [
            pltpu.VMEM((count, WIDE, 2 * HD), jnp.bfloat16),
            pltpu.SemaphoreType.DMA((count + len(later),)),
        ]
    specs += [IN_VMEM] * (len(operands) - len(specs))
    results = pl.pallas_call(
        functools.partial(project_kernel, spans, shifts, later, held, first, last),
        in_specs=specs,
        out_specs=[IN_VMEM] * len(shapes),
        out_shape=shapes,
        scratch_shapes=scratch,
        compiler_params=pltpu.CompilerParams(vmem_limit_bytes=VMEM),
        cost_estimate=pl.CostEstimate(
            flops=count * BOTH * WIDE * 512,
            bytes_accessed=count * 1100000,
            transcendentals=0,
        ),
    )(*operands)
    return (tuple(results[:2]), results[2]) if later else tuple(results)


def attend(queries, keys, values, allowed, guard, top_ref, mixed_ref, rows, active=None):
    parts = []
    highest = None
    for number in range(len(keys)):
        scores = lax.dot_general(
            queries, keys[number], (((1,), (1,)), ((), ())), preferred_element_type=jnp.float32
        )
        scores = scores * SCALE
        if allowed is not None:
            scores = jnp.where(allowed[number], scores, LOWEST)
        parts.append(scores)
        for begin in range(0, scores.shape[1], HD):
            piece = scores[:, begin : begin + HD]
            highest = piece if highest is None else jnp.maximum(highest, piece)
    before = top_ref[rows, :]
    top = jnp.maximum(before, jnp.max(highest, axis=1, keepdims=True))
    factor = jnp.exp2(before - top)
    earlier = mixed_ref[rows, :]
    mixed = earlier * jnp.concatenate([factor, factor], axis=1)
    for number in range(len(keys)):
        width = parts[number].shape[1]
        lifted = jnp.concatenate([top] * (width // HD), axis=1)
        weight = jnp.exp2(parts[number] - lifted)
        if guard:
            weight = jnp.where(allowed[number], weight, 0.0)
        mixed = mixed + jnp.dot(
            weight.astype(jnp.bfloat16), values[number], preferred_element_type=jnp.float32
        )
    if active is not None:
        top, mixed = jnp.where(active, top, before), jnp.where(active, mixed, earlier)
    top_ref[rows, :] = top
    mixed_ref[rows, :] = mixed


def per_row(table, begin):
    seat = lax.broadcasted_iota(jnp.int32, (ROW, HD), 0)
    found = jnp.zeros((ROW, HD), jnp.int32)
    for row in range(ROW):
        found = jnp.where(seat == row, table[begin + row], found)
    return found


def head_rows(pack):
    rows = pack[TOK : TOK + ROW, :]
    return [rows[:, head * HD : (head + 1) * HD] for head in range(GROUP)]


def reach_of(pack):
    coded = pack[TOK + ROW :, : 2 * HD].astype(jnp.float32)
    return coded[:, :HD] * 64.0 + coded[:, HD:]


def diagonal():
    row = lax.broadcasted_iota(jnp.int32, (HD, HD), 0)
    return row == lax.broadcasted_iota(jnp.int32, (HD, HD), 1)


def seal(top_ref, mixed_ref, begin, count, to, packed, levels):
    rows = slice(begin, begin + count)
    mixed = mixed_ref[rows, :]
    amount = mixed[:, HD:]
    some = amount > 0.0
    safe = jnp.where(some, amount, 1.0)
    packed[to : to + count, :] = (mixed[:, :HD] / safe).astype(jnp.bfloat16)
    level = jnp.where(some, top_ref[rows, :] + jnp.log2(safe), LOWEST)
    seat = lax.broadcasted_iota(jnp.int32, levels.shape, 0)
    for start in range(0, count, HD):
        flat = jnp.sum(
            jnp.where(diagonal(), level[start : start + HD, :], 0.0), axis=0, keepdims=True
        )
        levels = jnp.where(seat == (to + start) // HD, flat, levels)
    return levels


def stage_kernel(plan, place_ref, *refs):
    refs = list(refs)
    init, finish, extra = plan["init"], plan["finish"], plan["extra"]
    own, mate, carrier = plan["own"], plan["mate"], plan["carrier"]
    rows_too = carrier is not None or extra
    node_ref = refs.pop(0) if extra else None
    blocks = [refs.pop(0) for _ in plan["counts"]]
    own_pack = refs.pop(0)
    mate_pack = refs.pop(0) if mate or rows_too else None
    if extra:
        rim, row_pairs = refs.pop(0), refs.pop(0)
    if not init:
        refs = refs[2 * (own + mate + rows_too) :]
    packed = refs.pop(0) if finish else None
    if own:
        own_top, own_mixed = refs.pop(0), refs.pop(0)
    if mate:
        mate_top, mate_mixed = refs.pop(0), refs.pop(0)
    if rows_too:
        rows_top, rows_mixed = refs.pop(0), refs.pop(0)
    keys, values, decode_query, numbers = refs
    place = place_ref[0]
    mate_place = place + RUN - 2 * RUN * ((place // RUN) % 2)
    y, z = (place // RUN) % RING_Y, (place // (RING_Y * RUN)) * RUN + place % RUN
    size = plan["size"]
    bound = mate_place if mate else place
    ones = jnp.ones((TOK, HD), jnp.bfloat16)

    def span_of(slot):
        return pl.ds(pl.multiple_of(slot * TOK, TOK), TOK)

    slot, count, raw = 0, jnp.int32(0), []
    for block, amount in zip(blocks, plan["counts"]):
        for part in range(amount):
            dz, other = plan["offsets"][slot]
            far_y, far_z = (RING_Y - 1 - y) if other else y, (z + dz + RING_Z) % RING_Z
            number = (far_z // RUN) * (RING_Y * RUN) + far_y * RUN + far_z % RUN
            numbers[slot] = number
            key = block[part * TOK : (part + 1) * TOK, :HD]
            value = jnp.concatenate([block[part * TOK : (part + 1) * TOK, HD:], ones], axis=1)
            raw.append((key, value))
            keys[span_of(count), :] = key
            values[span_of(count), :] = value
            count = count + (number < bound).astype(jnp.int32)
            slot += 1
    if not (init and own):
        for more in range(size - 1):
            keys[span_of(count + more), :] = keys[:TOK, :]
            values[span_of(count + more), :] = jnp.zeros((TOK, 2 * HD), jnp.bfloat16)

    if rows_too:
        decode_query[...] = jnp.concatenate(head_rows(own_pack) + head_rows(mate_pack), axis=0)
    if carrier is not None:
        own_reach, mate_reach = reach_of(own_pack), reach_of(mate_pack)
        lane = lax.broadcasted_iota(jnp.int32, (ROW, TOK), 1).astype(jnp.float32)

    def decode(side):
        reach = jnp.where(side == 0, own_reach, mate_reach)
        allowed = []
        for slot in range(len(plan["offsets"])):
            left = reach - (numbers[slot] * TOK).astype(jnp.float32)
            fits = lane < jnp.concatenate([left, left], axis=1)
            allowed.append(jnp.concatenate([fits] * GROUP, axis=0))
        rows = pl.ds(pl.multiple_of(side * GROUP * ROW, GROUP * ROW), GROUP * ROW)
        attend(
            decode_query[rows, :],
            [key for key, _ in raw],
            [value for _, value in raw],
            allowed,
            True,
            rows_top,
            rows_mixed,
            rows,
        )

    def prefill(pack, some_keys, some_values, allowed, top_ref, mixed_ref, at_once, active=None):
        def some_heads(turn, carry):
            for number in range(at_once):
                head = turn * at_once + number
                lanes = pl.ds(pl.multiple_of(head * HD, HD), HD)
                attend(
                    pack[pl.ds(0, TOK), lanes],
                    some_keys,
                    some_values,
                    allowed,
                    False,
                    top_ref,
                    mixed_ref,
                    pl.ds(pl.multiple_of(head * TOK, TOK), TOK),
                    active,
                )
            if carrier is not None:
                for number in range(2 * at_once // GROUP):
                    decode(turn * 2 * at_once // GROUP + number)
            return carry

        if at_once == GROUP:
            some_heads(0, 0)
        else:
            lax.fori_loop(0, GROUP // at_once, some_heads, 0)

    fresh = [(own_top, own_mixed)] if init and own else []
    fresh += [(mate_top, mate_mixed), (rows_top, rows_mixed)] if init and mate else []
    for top_ref, mixed_ref in fresh:
        top_ref[...] = jnp.full(top_ref.shape, LOWEST, jnp.float32)
        mixed_ref[...] = jnp.zeros(mixed_ref.shape, jnp.float32)
    if init and own:
        token = lax.broadcasted_iota(jnp.int32, (TOK, TOK), 0)
        causal = [lax.broadcasted_iota(jnp.int32, (TOK, TOK), 1) <= token]
        prefill(own_pack, [keys[:TOK, :]], [values[:TOK, :]], causal, own_top, own_mixed, 4)
    else:
        pack = mate_pack if mate else own_pack
        top_ref, mixed_ref = (mate_top, mate_mixed) if mate else (own_top, own_mixed)

        def turn(number, carry, active=None):
            spans = [span_of(number * size + i) for i in range(size)]
            some_keys = [keys[span, :] for span in spans]
            some_values = [values[span, :] for span in spans]
            at_once = plan["at_once"]
            prefill(pack, some_keys, some_values, None, top_ref, mixed_ref, at_once, active)
            return carry

        if carrier is None:
            lax.fori_loop(0, (count + size - 1) // size, turn, 0)
        else:
            turn(0, 0, count > 0)

    if extra:
        nodes = per_row(node_ref, place * ROW)
        seat = lax.broadcasted_iota(jnp.int32, (ROW, HD), 0)
        column = lax.broadcasted_iota(jnp.int32, (ROW, HD), 1)
        key_nodes = jnp.full((ROW, HD), -1, jnp.int32)
        previous = jnp.maximum(place - 1, 0) * ROW
        for row in range(ROW):
            rim_node = jnp.where(place > 0, node_ref[previous + row], -1)
            key_nodes = jnp.where(column == row, rim_node, key_nodes)
            key_nodes = jnp.where(column == ROW + row, node_ref[place * ROW + row], key_nodes)
        same = (key_nodes == nodes) & (column <= seat + ROW)
        pad = jnp.zeros((HD - 2 * ROW, HD), jnp.bfloat16)
        extra_ones = jnp.ones((HD, HD), jnp.bfloat16)
        extra_keys = jnp.concatenate([rim[:, :HD], row_pairs[:, :HD], pad], axis=0)
        extra_values = jnp.concatenate([rim[:, HD:], row_pairs[:, HD:], pad], axis=0)
        attend(
            decode_query[: GROUP * ROW, :],
            [extra_keys],
            [jnp.concatenate([extra_values, extra_ones], axis=1)],
            [jnp.concatenate([same] * GROUP, axis=0)],
            True,
            rows_top,
            rows_mixed,
            slice(0, GROUP * ROW),
        )

    if finish:
        levels = jnp.zeros((LEVELS, HD), jnp.float32)
        for head in range(GROUP):
            levels = seal(mate_top, mate_mixed, head * TOK, TOK, head * TOK, packed, levels)
        levels = seal(rows_top, rows_mixed, GROUP * ROW, HD, GROUP * TOK, packed, levels)
        for part in range(3):
            rounded = levels.astype(jnp.bfloat16)
            begin = HEIGHT + part * LEVELS
            packed[begin : begin + LEVELS, :] = rounded
            levels = levels - rounded.astype(jnp.float32)


def stage(
    place,
    packs,
    blocks,
    offsets,
    state,
    init=False,
    own=False,
    mate=False,
    carrier=None,
    finish=False,
    extra=None,
    at_once=4,
    size=5,
):
    rows_too = carrier is not None or extra is not None
    plan = dict(
        counts=[block.shape[0] // TOK for block in blocks],
        offsets=offsets,
        init=init,
        own=own,
        mate=mate,
        carrier=carrier,
        finish=finish,
        extra=extra is not None,
        at_once=at_once,
        size=size,
    )
    total = len(offsets)
    smem = [place] + ([extra[0]] if extra else [])
    packs = list(packs) if mate or rows_too else [packs[0]]
    operands = smem + list(blocks) + packs + (list(extra[1:]) if extra else [])
    used = [name for name, flag in (("own", own), ("mate", mate), ("rows", rows_too)) if flag]
    sizes = dict(own=GROUP * TOK, mate=GROUP * TOK, rows=2 * GROUP * ROW)
    shapes = [jax.ShapeDtypeStruct((HEIGHT + 3 * LEVELS, HD), jnp.bfloat16)] if finish else []
    aliases = {}
    for name in used:
        for index, width in enumerate((HD, 2 * HD)):
            if not init:
                aliases[len(operands)] = len(shapes)
                operands.append(state[name][index])
            shapes.append(jax.ShapeDtypeStruct((sizes[name], width), jnp.float32))
    work = total * TOK * TOK * GROUP * (own + mate)
    results = pl.pallas_call(
        functools.partial(stage_kernel, plan),
        in_specs=[IN_SMEM] * len(smem) + [IN_VMEM] * (len(operands) - len(smem)),
        out_specs=[IN_VMEM] * len(shapes),
        out_shape=shapes,
        scratch_shapes=[
            pltpu.VMEM(((total + size) * TOK, HD), jnp.bfloat16),
            pltpu.VMEM(((total + size) * TOK, 2 * HD), jnp.bfloat16),
            pltpu.VMEM((2 * GROUP * ROW, HD), jnp.bfloat16),
            pltpu.SMEM((16,), jnp.int32),
        ],
        input_output_aliases=aliases,
        compiler_params=pltpu.CompilerParams(vmem_limit_bytes=VMEM),
        cost_estimate=pl.CostEstimate(
            flops=work * 8 * HD, bytes_accessed=2000000, transcendentals=work
        ),
    )(*operands)
    results = list(results)
    packed = results.pop(0) if finish else None
    state = dict(state or {})
    for name in used:
        state[name] = (results.pop(0), results.pop(0))
    return (state, packed) if finish else state


def merge_kernel(own_top, own_mixed, rows_top, rows_mixed, packed, out, out_rows):
    levels = jnp.zeros((LEVELS, HD), jnp.float32)
    for part in range(3):
        begin = HEIGHT + part * LEVELS
        levels = levels + packed[begin : begin + LEVELS, :].astype(jnp.float32)

    def joined(top_ref, mixed_ref, begin, at):
        rows = slice(begin, begin + HD)
        flat = levels[at // HD : at // HD + 1, :]
        level = jnp.sum(jnp.where(diagonal(), flat, 0.0), axis=1, keepdims=True)
        top = top_ref[rows, :]
        highest = jnp.maximum(top, level)
        mine, theirs = jnp.exp2(top - highest), jnp.exp2(level - highest)
        mixed = mixed_ref[rows, :]
        other = packed[at : at + HD, :].astype(jnp.float32)
        amount = mine * mixed[:, HD:] + theirs
        return ((mine * mixed[:, :HD] + theirs * other) / amount).astype(jnp.bfloat16)

    for head in range(GROUP):
        for start in range(0, TOK, HD):
            begin = head * TOK + start
            part = joined(own_top, own_mixed, begin, begin)
            out[start : start + HD, head * HD : (head + 1) * HD] = part
    part = joined(rows_top, rows_mixed, 0, GROUP * TOK)
    for head in range(GROUP):
        out_rows[:, head * HD : (head + 1) * HD] = part[head * ROW : (head + 1) * ROW, :]


def merge(state, packed):
    return pl.pallas_call(
        merge_kernel,
        in_specs=[IN_VMEM] * 5,
        out_specs=[IN_VMEM] * 2,
        out_shape=[
            jax.ShapeDtypeStruct((TOK, GROUP * HD), jnp.bfloat16),
            jax.ShapeDtypeStruct((ROW, GROUP * HD), jnp.bfloat16),
        ],
        compiler_params=pltpu.CompilerParams(vmem_limit_bytes=VMEM),
    )(*state["own"], *state["rows"], packed)


def per_device(
    hidden_context,
    hidden_rows,
    norm_gain,
    key_value_weight,
    value_bias,
    query_context,
    query_rows,
    context_length,
    row_node,
):
    weights = key_value_weight.reshape(D, 2 * HD)
    gain = norm_gain.reshape(8, WIDE)
    bias = value_bias.reshape(1, HD)
    tp = lax.axis_index("tp").astype(jnp.int32).reshape(1)
    place = lax.axis_index(PLACE).astype(jnp.int32).reshape(1)

    def swap(block, bits):
        return lax.ppermute(block, PLACE, [(i, i ^ bits) for i in range(32)])

    own = jnp.concatenate([hidden_context, hidden_rows], axis=0)
    low, high, twin = move_x(own, 1), move_x(own, -1), swap_core(own)
    digits = jnp.stack([context_length // 64, context_length % 64], axis=1)
    coded = jnp.repeat(digits.astype(jnp.bfloat16), HD, axis=1)
    coded = jnp.pad(coded, ((0, 0), (0, WIDE - 2 * HD)))
    own_pack = jnp.concatenate([query_context, query_rows, coded], axis=0)
    add = functools.partial(project, tp, gain)
    state = add(
        [[(hidden_context, 0, TOK), (hidden_rows, 0, ROW)], [(twin, 0, BOTH)]],
        [(0, 0), (0, 1)],
        weights,
    )
    low, high, state, own_pack = lax.optimization_barrier((low, high, state, own_pack))
    mate_pack = swap(own_pack, RUN)
    far_low, far_high = move_x(low[:TOP], 1), move_x(high[TOP:], -1)
    low_twin, high_twin = swap_core(low), swap_core(high)
    state, rest = add(
        [[(piece, 0, BOTH)] for piece in (low, high, low_twin, high_twin)],
        [(-1, 0), (1, 0), (-1, 1), (1, 1)],
        weights,
        later=[(2, 0), (2, 1)],
        state=state,
    )
    far_low, far_high, state, rest = lax.optimization_barrier((far_low, far_high, state, rest))
    far_twin = swap_core(jnp.concatenate([far_low, far_high], axis=0))
    far = [(far_low, 0, TOP), (far_high, 0, BOTH - TOP)]
    state = add([far], [(2, 0)], rest, held=[0], state=state)
    pairs, row_pairs = add(
        [[(far_twin, 0, BOTH)]], [(2, 1)], rest, held=[1], state=state, bias=bias
    )

    opposite = 3 * RUN
    run = functools.partial(stage, place, (own_pack, mate_pack))
    above, below = move(pairs, 1, 0), move(pairs, -1, 0)
    state = run([pairs], [(0, 0)], None, init=True, own=True)
    rim = lax.ppermute(row_pairs, PLACE, [(i, i + 1) for i in range(31)])
    above, below, state, rim = lax.optimization_barrier((above, below, state, rim))
    above_two, below_two = move(above, 1, 0), move(below, -1, 0)
    first = swap(jnp.concatenate([pairs, above, below], axis=0), opposite)
    above_two, below_two, mate_pack = lax.optimization_barrier((above_two, below_two, mate_pack))
    run = functools.partial(stage, place, (own_pack, mate_pack))
    above_three, below_three = move(above_two, 1, 0), move(below_two, -1, 0)
    second = swap(jnp.concatenate([above_two, below_two], axis=0), opposite)
    line = [pairs, above, below, above_two, below_two]
    steps = [(0, 0), (-1, 0), (1, 0), (-2, 0), (2, 0)]
    state = run(line, steps, state, init=True, mate=True, carrier="mate")
    above_three, below_three, state = lax.optimization_barrier((above_three, below_three, state))
    ends = [move(above_three[:TOP], 1, 0), move(below_three[TOP:], -1, 0)]
    third = swap(jnp.concatenate([above_three, below_three], axis=0), opposite)
    across = [first, second]
    across_steps = [(0, 1), (-1, 1), (1, 1), (-2, 1), (2, 1)]
    state = run(across, across_steps, state, mate=True, carrier="mate", at_once=GROUP)
    ends, state = lax.optimization_barrier((ends, state))
    end = jnp.concatenate(ends, axis=0)
    fourth = swap(end, opposite)
    late, late_steps = [above_three, below_three, end], [(-3, 0), (3, 0), (4, 0)]
    state = run(late, late_steps, state, mate=True, carrier="mate", size=3)
    last, last_steps = [third, fourth], [(-3, 1), (3, 1), (4, 1)]
    state, packed = run(last, last_steps, state, mate=True, carrier="mate", finish=True, size=3, at_once=GROUP)
    sent = swap(packed, RUN)
    packed, state = lax.optimization_barrier((packed, state))
    state = run(
        line[1:] + across + late + last,
        steps[1:] + across_steps + late_steps + last_steps,
        state,
        own=True,
        extra=(row_node, rim, row_pairs),
        at_once=GROUP,
    )
    out, out_rows = merge(state, sent)
    return out, out_rows


def solution(mesh):
    return jax.shard_map(
        per_device,
        mesh=mesh,
        in_specs=(
            P(PLACE, "tp"),
            P(PLACE, "tp"),
            P(),
            P(None, None, "tp"),
            P("tp"),
            P(PLACE, "tp"),
            P(PLACE, "tp"),
            P(PLACE),
            P(),
        ),
        out_specs=(P(PLACE, "tp"), P(PLACE, "tp")),
        check_vma=False,
    )
```

```python
import functools
import math

import jax
import jax.numpy as jnp
from jax import lax
from jax.experimental import pallas as pl
from jax.experimental.pallas import tpu as pltpu
from jax.sharding import PartitionSpec as P

D = 8192
H = 64
KVH = 8
HD = 128
STEPS = 4
GROUP = H // KVH

PLACE = ("sec", "seq")
RING_Z, RING_Y, RUN = 8, 4, 4
TOK = 256
ROW = 16
BOTH = TOK + ROW
TOP = 128
WIDE = 1024
HEIGHT = GROUP * (TOK + ROW)
LEVELS = 32
LOWEST = -1e30
SCALE = math.log2(math.e) / math.sqrt(HD)
VMEM = 32 * 1024 * 1024
IN_VMEM = pl.BlockSpec(memory_space=pltpu.VMEM)
IN_SMEM = pl.BlockSpec(memory_space=pltpu.SMEM)
IN_HBM = pl.BlockSpec(memory_space=pltpu.HBM)


def place_of(y, z):
    return (z // RUN) * (RING_Y * RUN) + y * RUN + z % RUN


def move(block, dz, dy):
    route = [
        (place_of(y, z), place_of((y + dy) % RING_Y, (z + dz) % RING_Z))
        for y in range(RING_Y)
        for z in range(RING_Z)
    ]
    return lax.ppermute(block, PLACE, route)


def move_x(block, step):
    return lax.ppermute(block, "tp", [(i, (i + 2 * step) % 8) for i in range(8)])


def swap_core(block):
    return lax.ppermute(block, "tp", [(i, i ^ 1) for i in range(8)])


def project_kernel(spans, shifts, later, held, first, last, tp_ref, *refs):
    refs = list(refs)
    pieces = [[(refs.pop(0), *span) for span in piece] for piece in spans]
    weights, gain = refs.pop(0), refs.pop(0)
    if not first:
        product_in, squares_in = refs.pop(0), refs.pop(0)
    if last:
        bias = refs.pop(0)
    tp = tp_ref[0]
    mate = tp + 1 - 2 * (tp % 2)

    def owner_of(shift):
        step, other = shift
        return ((mate if other else tp) + 2 * step + 8) % 8

    copies = []
    if held is None:
        ready, slices = refs.pop(), refs.pop()
        for number, shift in enumerate(shifts + later):
            rows = pl.ds(pl.multiple_of(owner_of(shift) * WIDE, WIDE), WIDE)
            far = number - len(shifts)
            to = slices.at[number] if far < 0 else refs[2].at[far]
            copies.append(pltpu.make_async_copy(weights.at[rows, :], to, ready.at[number]))
            copies[-1].start()
    else:
        slices = weights
    product = jnp.zeros((BOTH, 2 * HD), jnp.float32) if first else product_in[...]
    squares = jnp.zeros((BOTH, HD), jnp.float32) if first else squares_in[...]
    for number, (piece, shift) in enumerate(zip(pieces, shifts)):
        if held is None:
            copies[number].wait()
        slot = number if held is None else held[number]

        def chunk(turn, carry, piece=piece, slot=slot, owner=owner_of(shift)):
            product, squares = carry
            span = pl.ds(pl.multiple_of(turn * 256, 256), 256)
            chunks = [ref[pl.ds(start, stop - start), span] for ref, start, stop in piece]
            wide = jnp.concatenate(chunks, axis=0).astype(jnp.float32)
            squared = wide * wide
            squares = squares + (squared[:, :HD] + squared[:, HD:])
            scaled = (wide * gain[pl.ds(owner, 1), span]).astype(jnp.bfloat16)
            return (
                product
                + jnp.dot(scaled, slices[slot, span, :], preferred_element_type=jnp.float32),
                squares,
            )

        if len(pieces) == 1:
            for number in range(WIDE // 256):
                product, squares = chunk(number, (product, squares))
        else:
            product, squares = lax.fori_loop(0, WIDE // 256, chunk, (product, squares))
    for copy in copies[len(shifts) :]:
        copy.wait()
    if not last:
        refs[0][...] = product
        refs[1][...] = squares
        return
    inverse = lax.rsqrt(jnp.sum(squares, axis=1, keepdims=True) / D + 1e-06)
    keys = (product[:, :HD] * inverse).astype(jnp.bfloat16)
    values = (product[:, HD:] * inverse + bias[...]).astype(jnp.bfloat16)
    refs[0][:, :HD] = keys[:TOK]
    refs[0][:, HD:] = values[:TOK]
    refs[1][:, :HD] = keys[TOK:]
    refs[1][:, HD:] = values[TOK:]


def project(tp, gain, pieces, shifts, weights, later=(), held=None, state=None, bias=None):
    spans = [[(start, stop) for _, start, stop in piece] for piece in pieces]
    count, later = len(pieces), list(later)
    first, last = state is None, bias is not None
    operands = [tp] + [chunk[0] for piece in pieces for chunk in piece] + [weights, gain]
    specs = [IN_SMEM] + [IN_VMEM] * (len(operands) - 3)
    specs += [IN_HBM if held is None else IN_VMEM, IN_VMEM]
    if not first:
        operands += list(state)
    if last:
        operands.append(bias)
        shapes = [
            jax.ShapeDtypeStruct((TOK, 2 * HD), jnp.bfloat16),
            jax.ShapeDtypeStruct((ROW, 2 * HD), jnp.bfloat16),
        ]
    else:
        shapes = [
            jax.ShapeDtypeStruct((BOTH, 2 * HD), jnp.float32),
            jax.ShapeDtypeStruct((BOTH, HD), jnp.float32),
        ]
    if later:
        shapes.append(jax.ShapeDtypeStruct((len(later), WIDE, 2 * HD), jnp.bfloat16))
    scratch = []
    if held is None:
        scratch = [
            pltpu.VMEM((count, WIDE, 2 * HD), jnp.bfloat16),
            pltpu.SemaphoreType.DMA((count + len(later),)),
        ]
    specs += [IN_VMEM] * (len(operands) - len(specs))
    results = pl.pallas_call(
        functools.partial(project_kernel, spans, shifts, later, held, first, last),
        in_specs=specs,
        out_specs=[IN_VMEM] * len(shapes),
        out_shape=shapes,
        scratch_shapes=scratch,
        compiler_params=pltpu.CompilerParams(vmem_limit_bytes=VMEM),
        cost_estimate=pl.CostEstimate(
            flops=count * BOTH * WIDE * 512,
            bytes_accessed=count * 1100000,
            transcendentals=0,
        ),
    )(*operands)
    return (tuple(results[:2]), results[2]) if later else tuple(results)


def attend(queries, keys, values, allowed, guard, top_ref, mixed_ref, rows, active=None):
    parts = []
    highest = None
    for number in range(len(keys)):
        scores = lax.dot_general(
            queries, keys[number], (((1,), (1,)), ((), ())), preferred_element_type=jnp.float32
        )
        scores = scores * SCALE
        if allowed is not None:
            scores = jnp.where(allowed[number], scores, LOWEST)
        parts.append(scores)
        for begin in range(0, scores.shape[1], HD):
            piece = scores[:, begin : begin + HD]
            highest = piece if highest is None else jnp.maximum(highest, piece)
    before = top_ref[rows, :]
    top = jnp.maximum(before, jnp.max(highest, axis=1, keepdims=True))
    factor = jnp.exp2(before - top)
    earlier = mixed_ref[rows, :]
    mixed = earlier * jnp.concatenate([factor, factor], axis=1)
    for number in range(len(keys)):
        width = parts[number].shape[1]
        lifted = jnp.concatenate([top] * (width // HD), axis=1)
        weight = jnp.exp2(parts[number] - lifted)
        if guard:
            weight = jnp.where(allowed[number], weight, 0.0)
        mixed = mixed + jnp.dot(
            weight.astype(jnp.bfloat16), values[number], preferred_element_type=jnp.float32
        )
    if active is not None:
        top, mixed = jnp.where(active, top, before), jnp.where(active, mixed, earlier)
    top_ref[rows, :] = top
    mixed_ref[rows, :] = mixed


def per_row(table, begin):
    seat = lax.broadcasted_iota(jnp.int32, (ROW, HD), 0)
    found = jnp.zeros((ROW, HD), jnp.int32)
    for row in range(ROW):
        found = jnp.where(seat == row, table[begin + row], found)
    return found


def head_rows(pack):
    rows = pack[TOK : TOK + ROW, :]
    return [rows[:, head * HD : (head + 1) * HD] for head in range(GROUP)]


def reach_of(pack):
    coded = pack[TOK + ROW :, : 2 * HD].astype(jnp.float32)
    return coded[:, :HD] * 64.0 + coded[:, HD:]


def diagonal():
    row = lax.broadcasted_iota(jnp.int32, (HD, HD), 0)
    return row == lax.broadcasted_iota(jnp.int32, (HD, HD), 1)


def seal(top_ref, mixed_ref, begin, count, to, packed, levels):
    rows = slice(begin, begin + count)
    mixed = mixed_ref[rows, :]
    amount = mixed[:, HD:]
    some = amount > 0.0
    safe = jnp.where(some, amount, 1.0)
    packed[to : to + count, :] = (mixed[:, :HD] / safe).astype(jnp.bfloat16)
    level = jnp.where(some, top_ref[rows, :] + jnp.log2(safe), LOWEST)
    seat = lax.broadcasted_iota(jnp.int32, levels.shape, 0)
    for start in range(0, count, HD):
        flat = jnp.sum(
            jnp.where(diagonal(), level[start : start + HD, :], 0.0), axis=0, keepdims=True
        )
        levels = jnp.where(seat == (to + start) // HD, flat, levels)
    return levels


def stage_kernel(plan, place_ref, *refs):
    refs = list(refs)
    init, finish, extra = plan["init"], plan["finish"], plan["extra"]
    own, mate, carrier = plan["own"], plan["mate"], plan["carrier"]
    rows_too = carrier is not None or extra
    node_ref = refs.pop(0) if extra else None
    blocks = [refs.pop(0) for _ in plan["counts"]]
    own_pack = refs.pop(0)
    mate_pack = refs.pop(0) if mate or rows_too else None
    if extra:
        rim, row_pairs = refs.pop(0), refs.pop(0)
    if not init:
        refs = refs[2 * (own + mate + rows_too) :]
    packed = refs.pop(0) if finish else None
    if own:
        own_top, own_mixed = refs.pop(0), refs.pop(0)
    if mate:
        mate_top, mate_mixed = refs.pop(0), refs.pop(0)
    if rows_too:
        rows_top, rows_mixed = refs.pop(0), refs.pop(0)
    keys, values, decode_query, numbers = refs
    place = place_ref[0]
    mate_place = place + RUN - 2 * RUN * ((place // RUN) % 2)
    y, z = (place // RUN) % RING_Y, (place // (RING_Y * RUN)) * RUN + place % RUN
    size = plan["size"]
    bound = mate_place if mate else place
    ones = jnp.ones((TOK, HD), jnp.bfloat16)

    def span_of(slot):
        return pl.ds(pl.multiple_of(slot * TOK, TOK), TOK)

    slot, count, raw = 0, jnp.int32(0), []
    for block, amount in zip(blocks, plan["counts"]):
        for part in range(amount):
            dz, other = plan["offsets"][slot]
            far_y, far_z = (RING_Y - 1 - y) if other else y, (z + dz + RING_Z) % RING_Z
            number = (far_z // RUN) * (RING_Y * RUN) + far_y * RUN + far_z % RUN
            numbers[slot] = number
            key = block[part * TOK : (part + 1) * TOK, :HD]
            value = jnp.concatenate([block[part * TOK : (part + 1) * TOK, HD:], ones], axis=1)
            raw.append((key, value))
            keys[span_of(count), :] = key
            values[span_of(count), :] = value
            count = count + (number < bound).astype(jnp.int32)
            slot += 1
    if not (init and own):
        for more in range(size - 1):
            keys[span_of(count + more), :] = keys[:TOK, :]
            values[span_of(count + more), :] = jnp.zeros((TOK, 2 * HD), jnp.bfloat16)

    if rows_too:
        decode_query[...] = jnp.concatenate(head_rows(own_pack) + head_rows(mate_pack), axis=0)
    if carrier is not None:
        own_reach, mate_reach = reach_of(own_pack), reach_of(mate_pack)
        lane = lax.broadcasted_iota(jnp.int32, (ROW, TOK), 1).astype(jnp.float32)

    def decode(side):
        reach = jnp.where(side == 0, own_reach, mate_reach)
        allowed = []
        for slot in range(len(plan["offsets"])):
            left = reach - (numbers[slot] * TOK).astype(jnp.float32)
            fits = lane < jnp.concatenate([left, left], axis=1)
            allowed.append(jnp.concatenate([fits] * GROUP, axis=0))
        rows = pl.ds(pl.multiple_of(side * GROUP * ROW, GROUP * ROW), GROUP * ROW)
        attend(
            decode_query[rows, :],
            [key for key, _ in raw],
            [value for _, value in raw],
            allowed,
            True,
            rows_top,
            rows_mixed,
            rows,
        )

    def prefill(pack, some_keys, some_values, allowed, top_ref, mixed_ref, at_once, active=None):
        def some_heads(turn, carry):
            for number in range(at_once):
                head = turn * at_once + number
                lanes = pl.ds(pl.multiple_of(head * HD, HD), HD)
                attend(
                    pack[pl.ds(0, TOK), lanes],
                    some_keys,
                    some_values,
                    allowed,
                    False,
                    top_ref,
                    mixed_ref,
                    pl.ds(pl.multiple_of(head * TOK, TOK), TOK),
                    active,
                )
            if carrier is not None:
                for number in range(2 * at_once // GROUP):
                    decode(turn * 2 * at_once // GROUP + number)
            return carry

        if at_once == GROUP:
            some_heads(0, 0)
        else:
            lax.fori_loop(0, GROUP // at_once, some_heads, 0)

    fresh = [(own_top, own_mixed)] if init and own else []
    fresh += [(mate_top, mate_mixed), (rows_top, rows_mixed)] if init and mate else []
    for top_ref, mixed_ref in fresh:
        top_ref[...] = jnp.full(top_ref.shape, LOWEST, jnp.float32)
        mixed_ref[...] = jnp.zeros(mixed_ref.shape, jnp.float32)
    if init and own:
        token = lax.broadcasted_iota(jnp.int32, (TOK, TOK), 0)
        causal = [lax.broadcasted_iota(jnp.int32, (TOK, TOK), 1) <= token]
        prefill(own_pack, [keys[:TOK, :]], [values[:TOK, :]], causal, own_top, own_mixed, 4)
    else:
        pack = mate_pack if mate else own_pack
        top_ref, mixed_ref = (mate_top, mate_mixed) if mate else (own_top, own_mixed)

        def turn(number, carry, active=None):
            spans = [span_of(number * size + i) for i in range(size)]
            some_keys = [keys[span, :] for span in spans]
            some_values = [values[span, :] for span in spans]
            at_once = plan["at_once"]
            prefill(pack, some_keys, some_values, None, top_ref, mixed_ref, at_once, active)
            return carry

        if carrier is None:
            lax.fori_loop(0, (count + size - 1) // size, turn, 0)
        else:
            turn(0, 0, count > 0)

    if extra:
        nodes = per_row(node_ref, place * ROW)
        seat = lax.broadcasted_iota(jnp.int32, (ROW, HD), 0)
        column = lax.broadcasted_iota(jnp.int32, (ROW, HD), 1)
        key_nodes = jnp.full((ROW, HD), -1, jnp.int32)
        previous = jnp.maximum(place - 1, 0) * ROW
        for row in range(ROW):
            rim_node = jnp.where(place > 0, node_ref[previous + row], -1)
            key_nodes = jnp.where(column == row, rim_node, key_nodes)
            key_nodes = jnp.where(column == ROW + row, node_ref[place * ROW + row], key_nodes)
        same = (key_nodes == nodes) & (column <= seat + ROW)
        pad = jnp.zeros((HD - 2 * ROW, HD), jnp.bfloat16)
        extra_ones = jnp.ones((HD, HD), jnp.bfloat16)
        extra_keys = jnp.concatenate([rim[:, :HD], row_pairs[:, :HD], pad], axis=0)
        extra_values = jnp.concatenate([rim[:, HD:], row_pairs[:, HD:], pad], axis=0)
        attend(
            decode_query[: GROUP * ROW, :],
            [extra_keys],
            [jnp.concatenate([extra_values, extra_ones], axis=1)],
            [jnp.concatenate([same] * GROUP, axis=0)],
            True,
            rows_top,
            rows_mixed,
            slice(0, GROUP * ROW),
        )

    if finish:
        levels = jnp.zeros((LEVELS, HD), jnp.float32)
        for head in range(GROUP):
            levels = seal(mate_top, mate_mixed, head * TOK, TOK, head * TOK, packed, levels)
        levels = seal(rows_top, rows_mixed, GROUP * ROW, HD, GROUP * TOK, packed, levels)
        for part in range(3):
            rounded = levels.astype(jnp.bfloat16)
            begin = HEIGHT + part * LEVELS
            packed[begin : begin + LEVELS, :] = rounded
            levels = levels - rounded.astype(jnp.float32)


def stage(
    place,
    packs,
    blocks,
    offsets,
    state,
    init=False,
    own=False,
    mate=False,
    carrier=None,
    finish=False,
    extra=None,
    at_once=4,
    size=5,
):
    rows_too = carrier is not None or extra is not None
    plan = dict(
        counts=[block.shape[0] // TOK for block in blocks],
        offsets=offsets,
        init=init,
        own=own,
        mate=mate,
        carrier=carrier,
        finish=finish,
        extra=extra is not None,
        at_once=at_once,
        size=size,
    )
    total = len(offsets)
    smem = [place] + ([extra[0]] if extra else [])
    packs = list(packs) if mate or rows_too else [packs[0]]
    operands = smem + list(blocks) + packs + (list(extra[1:]) if extra else [])
    used = [name for name, flag in (("own", own), ("mate", mate), ("rows", rows_too)) if flag]
    sizes = dict(own=GROUP * TOK, mate=GROUP * TOK, rows=2 * GROUP * ROW)
    shapes = [jax.ShapeDtypeStruct((HEIGHT + 3 * LEVELS, HD), jnp.bfloat16)] if finish else []
    aliases = {}
    for name in used:
        for index, width in enumerate((HD, 2 * HD)):
            if not init:
                aliases[len(operands)] = len(shapes)
                operands.append(state[name][index])
            shapes.append(jax.ShapeDtypeStruct((sizes[name], width), jnp.float32))
    work = total * TOK * TOK * GROUP * (own + mate)
    results = pl.pallas_call(
        functools.partial(stage_kernel, plan),
        in_specs=[IN_SMEM] * len(smem) + [IN_VMEM] * (len(operands) - len(smem)),
        out_specs=[IN_VMEM] * len(shapes),
        out_shape=shapes,
        scratch_shapes=[
            pltpu.VMEM(((total + size) * TOK, HD), jnp.bfloat16),
            pltpu.VMEM(((total + size) * TOK, 2 * HD), jnp.bfloat16),
            pltpu.VMEM((2 * GROUP * ROW, HD), jnp.bfloat16),
            pltpu.SMEM((16,), jnp.int32),
        ],
        input_output_aliases=aliases,
        compiler_params=pltpu.CompilerParams(vmem_limit_bytes=VMEM),
        cost_estimate=pl.CostEstimate(
            flops=work * 8 * HD, bytes_accessed=2000000, transcendentals=work
        ),
    )(*operands)
    results = list(results)
    packed = results.pop(0) if finish else None
    state = dict(state or {})
    for name in used:
        state[name] = (results.pop(0), results.pop(0))
    return (state, packed) if finish else state


def merge_kernel(own_top, own_mixed, rows_top, rows_mixed, packed, out, out_rows):
    levels = jnp.zeros((LEVELS, HD), jnp.float32)
    for part in range(3):
        begin = HEIGHT + part * LEVELS
        levels = levels + packed[begin : begin + LEVELS, :].astype(jnp.float32)

    def joined(top_ref, mixed_ref, begin, at):
        rows = slice(begin, begin + HD)
        flat = levels[at // HD : at // HD + 1, :]
        level = jnp.sum(jnp.where(diagonal(), flat, 0.0), axis=1, keepdims=True)
        top = top_ref[rows, :]
        highest = jnp.maximum(top, level)
        mine, theirs = jnp.exp2(top - highest), jnp.exp2(level - highest)
        mixed = mixed_ref[rows, :]
        other = packed[at : at + HD, :].astype(jnp.float32)
        amount = mine * mixed[:, HD:] + theirs
        return ((mine * mixed[:, :HD] + theirs * other) / amount).astype(jnp.bfloat16)

    for head in range(GROUP):
        for start in range(0, TOK, HD):
            begin = head * TOK + start
            part = joined(own_top, own_mixed, begin, begin)
            out[start : start + HD, head * HD : (head + 1) * HD] = part
    part = joined(rows_top, rows_mixed, 0, GROUP * TOK)
    for head in range(GROUP):
        out_rows[:, head * HD : (head + 1) * HD] = part[head * ROW : (head + 1) * ROW, :]


def merge(state, packed):
    return pl.pallas_call(
        merge_kernel,
        in_specs=[IN_VMEM] * 5,
        out_specs=[IN_VMEM] * 2,
        out_shape=[
            jax.ShapeDtypeStruct((TOK, GROUP * HD), jnp.bfloat16),
            jax.ShapeDtypeStruct((ROW, GROUP * HD), jnp.bfloat16),
        ],
        compiler_params=pltpu.CompilerParams(vmem_limit_bytes=VMEM),
    )(*state["own"], *state["rows"], packed)


def per_device(
    hidden_context,
    hidden_rows,
    norm_gain,
    key_value_weight,
    value_bias,
    query_context,
    query_rows,
    context_length,
    row_node,
):
    weights = key_value_weight.reshape(D, 2 * HD)
    gain = norm_gain.reshape(8, WIDE)
    bias = value_bias.reshape(1, HD)
    tp = lax.axis_index("tp").astype(jnp.int32).reshape(1)
    place = lax.axis_index(PLACE).astype(jnp.int32).reshape(1)

    def swap(block, bits):
        return lax.ppermute(block, PLACE, [(i, i ^ bits) for i in range(32)])

    own = jnp.concatenate([hidden_context, hidden_rows], axis=0)
    low, high, twin = move_x(own, 1), move_x(own, -1), swap_core(own)
    digits = jnp.stack([context_length // 64, context_length % 64], axis=1)
    coded = jnp.repeat(digits.astype(jnp.bfloat16), HD, axis=1)
    coded = jnp.pad(coded, ((0, 0), (0, WIDE - 2 * HD)))
    own_pack = jnp.concatenate([query_context, query_rows, coded], axis=0)
    add = functools.partial(project, tp, gain)
    state = add(
        [[(hidden_context, 0, TOK), (hidden_rows, 0, ROW)], [(twin, 0, BOTH)]],
        [(0, 0), (0, 1)],
        weights,
    )
    low, high, state, own_pack = lax.optimization_barrier((low, high, state, own_pack))
    mate_pack = swap(own_pack, RUN)
    far_low, far_high = move_x(low[:TOP], 1), move_x(high[TOP:], -1)
    low_twin, high_twin = swap_core(low), swap_core(high)
    state, rest = add(
        [[(piece, 0, BOTH)] for piece in (low, high, low_twin, high_twin)],
        [(-1, 0), (1, 0), (-1, 1), (1, 1)],
        weights,
        later=[(2, 0), (2, 1)],
        state=state,
    )
    far_low, far_high, state, rest = lax.optimization_barrier((far_low, far_high, state, rest))
    far_twin = swap_core(jnp.concatenate([far_low, far_high], axis=0))
    far = [(far_low, 0, TOP), (far_high, 0, BOTH - TOP)]
    state = add([far], [(2, 0)], rest, held=[0], state=state)
    pairs, row_pairs = add(
        [[(far_twin, 0, BOTH)]], [(2, 1)], rest, held=[1], state=state, bias=bias
    )

    opposite = 3 * RUN
    run = functools.partial(stage, place, (own_pack, mate_pack))
    above, below = move(pairs, 1, 0), move(pairs, -1, 0)
    state = run([pairs], [(0, 0)], None, init=True, own=True)
    above, below, state, row_pairs = lax.optimization_barrier((above, below, state, row_pairs))
    above_two, below_two = move(above, 1, 0), move(below, -1, 0)
    first = swap(jnp.concatenate([pairs, above, below], axis=0), opposite)
    rim = lax.ppermute(row_pairs, PLACE, [(i, i + 1) for i in range(31)])
    above_two, below_two, mate_pack, rim = lax.optimization_barrier(
        (above_two, below_two, mate_pack, rim)
    )
    run = functools.partial(stage, place, (own_pack, mate_pack))
    above_three, below_three = move(above_two, 1, 0), move(below_two, -1, 0)
    second = swap(jnp.concatenate([above_two, below_two], axis=0), opposite)
    line = [pairs, above, below, above_two, below_two]
    steps = [(0, 0), (-1, 0), (1, 0), (-2, 0), (2, 0)]
    state = run(line, steps, state, init=True, mate=True, carrier="mate")
    above_three, below_three, state = lax.optimization_barrier((above_three, below_three, state))
    ends = [move(above_three[:TOP], 1, 0), move(below_three[TOP:], -1, 0)]
    third = swap(jnp.concatenate([above_three, below_three], axis=0), opposite)
    across = [first, second]
    across_steps = [(0, 1), (-1, 1), (1, 1), (-2, 1), (2, 1)]
    state = run(across, across_steps, state, mate=True, carrier="mate", at_once=GROUP)
    ends, state = lax.optimization_barrier((ends, state))
    end = jnp.concatenate(ends, axis=0)
    fourth = swap(end, opposite)
    late, late_steps = [above_three, below_three, end], [(-3, 0), (3, 0), (4, 0)]
    state = run(late, late_steps, state, mate=True, carrier="mate", size=3)
    last, last_steps = [third, fourth], [(-3, 1), (3, 1), (4, 1)]
    state, packed = run(last, last_steps, state, mate=True, carrier="mate", finish=True, size=3, at_once=GROUP)
    sent = swap(packed, RUN)
    packed, state = lax.optimization_barrier((packed, state))
    state = run(
        line[1:] + across + late + last,
        steps[1:] + across_steps + late_steps + last_steps,
        state,
        own=True,
        extra=(row_node, rim, row_pairs),
        at_once=GROUP,
    )
    out, out_rows = merge(state, sent)
    return out, out_rows


def solution(mesh):
    return jax.shard_map(
        per_device,
        mesh=mesh,
        in_specs=(
            P(PLACE, "tp"),
            P(PLACE, "tp"),
            P(),
            P(None, None, "tp"),
            P("tp"),
            P(PLACE, "tp"),
            P(PLACE, "tp"),
            P(PLACE),
            P(),
        ),
        out_specs=(P(PLACE, "tp"), P(PLACE, "tp")),
        check_vma=False,
    )
```
